32 devices in a mesh: grp: 1, lat: 32 (over z, y, x, core).
Axes of the slice: x: 2, y: 2, z: 4, core: 2. Of those that a mesh axis runs over, the one named last changes fastest.
Arguments:
- fields: bfloat16 [768, 64, 2048], P(('grp', 'lat')), may hold values from -6 to 6
- spectral_weight: bfloat16 [2, 128, 64, 128], replicated, may hold values from -0.5 to 0.5
- local_weight: bfloat16 [2, 64, 64], replicated, may hold values from -0.75 to 0.75
Outputs:
- updated: bfloat16 [768, 64, 2048], P(('grp', 'lat'))
The draws below stay inside these ranges and needn't reach their ends.
All inputs are finite; a program needn't handle non-finite values.
Results may differ from the reference program's by a relative error of at most 0.011.
Values may be sent and summed in bfloat16 or wider, within the bound.
No kernel may reach another device: no remote copies, remote signals or barrier semaphores. Data moves between devices by JAX's collectives and lax.ppermute only.
A program may use at most 128 MiB of HBM per device.

```python
import math
import jax
import jax.numpy as jnp

C = 64
NLON = 2048
KX = 128
KY = 128
LAYERS = 2
ROWS_DEV = 24
NLAT = 768


def levels(stream_key, extent, split, low, largest):
    level = 1.0
    for position, shards_of in split:
        heights = jax.random.uniform(jax.random.fold_in(jax.random.fold_in(stream_key, 6), position), (shards_of,), jnp.float32, low / len(split), largest / len(split))
        level = level * jnp.repeat(jnp.exp(heights), extent[position] // shards_of).reshape((-1,) + (1,) * (len(extent) - 1 - position))
    return level


def centred(own_key, dims, spread, reach, split=(), kind=jnp.bfloat16):
    result = jax.random.normal(own_key, dims, jnp.float32) * spread
    if len(split) > 0:
        result = levels(own_key, dims, split, -0.22, 0.18) * result
    return jnp.clip(result, min=-reach, max=reach).astype(kind)


def setup_inputs(seed: int = 0, part: int = 0) -> dict:
    streams_of = jax.random.split(jax.random.key(seed), 4)
    part_keys = jax.random.split(jax.random.fold_in(streams_of[3], part), 4)
    fields = centred(part_keys[0], (NLAT, C, NLON), 1.0, 6.0, ((0, 32),))
    spectral_weight = centred(streams_of[1], (LAYERS, KX, C, 2 * C), (2 * C) ** -0.5, 0.5)
    local_weight = centred(streams_of[2], (LAYERS, C, C), C ** -0.5, 0.75)
    return {"fields": fields, "spectral_weight": spectral_weight, "local_weight": local_weight}


def lon_forward_table(lon_count, mode_count):
    cells = jnp.arange(lon_count, dtype=jnp.int32)[:, None]
    modes = jnp.arange(mode_count, dtype=jnp.int32)[None, :]
    angle = 2.0 * jnp.pi / lon_count * (cells * modes % lon_count).astype(jnp.float32)
    factor = 1.0 / math.sqrt(lon_count)
    return jnp.stack([jnp.cos(angle) * factor, -jnp.sin(angle) * factor], axis=1).astype(jnp.bfloat16)

def lon_back_table(lon_count, mode_count):
    modes = jnp.arange(mode_count, dtype=jnp.int32)[:, None]
    cells = jnp.arange(lon_count, dtype=jnp.int32)[None, :]
    angle = 2.0 * jnp.pi / lon_count * (cells * modes % lon_count).astype(jnp.float32)
    factor = 1.0 / math.sqrt(mode_count)
    return jnp.stack([jnp.cos(angle) * factor, -jnp.sin(angle) * factor], axis=1).astype(jnp.bfloat16)

def kept_wavenumbers(lat_count, kept_count):
    index = jnp.arange(kept_count, dtype=jnp.int32)
    return jnp.where(index < kept_count // 2, index, lat_count - kept_count + index).astype(jnp.int32)

def row_latitudes(lat_count, block_rows):
    rowids = jnp.arange(lat_count, dtype=jnp.int32)
    stride = lat_count // block_rows
    return (rowids % block_rows * stride + rowids // block_rows).astype(jnp.int32)

def lat_tables(lat_count, kept_count, block_rows):
    waves = kept_wavenumbers(lat_count, kept_count)
    latitudes = row_latitudes(lat_count, block_rows)
    angle = 2.0 * jnp.pi / lat_count * (waves[:, None] * latitudes[None, :] % lat_count).astype(jnp.float32)
    forward = jnp.stack([jnp.cos(angle), jnp.sin(angle)], axis=0) * (1.0 / math.sqrt(lat_count))
    backward = jnp.stack([jnp.cos(angle).T, jnp.sin(angle).T], axis=0) * (1.0 / math.sqrt(kept_count))
    return (forward.astype(jnp.bfloat16), backward.astype(jnp.bfloat16))

def lat_forward(table, values, channels):
    products = jnp.einsum('pjn,nkc->pjkc', table.astype(jnp.float32), values.astype(jnp.float32))
    real_part = products[0, ..., :channels] + products[1, ..., channels:]
    imag_part = products[0, ..., channels:] - products[1, ..., :channels]
    return jnp.concatenate([real_part, imag_part], axis=-1)

def lat_backward(table, modes, channels):
    products = jnp.einsum('pnj,jkc->pnkc', table.astype(jnp.float32), modes.astype(jnp.float32))
    real_part = products[0, ..., :channels] - products[1, ..., channels:]
    imag_part = products[1, ..., :channels] + products[0, ..., channels:]
    return jnp.concatenate([real_part, imag_part], axis=-1)

def mix_matrix(weight, channels):
    real_w = weight[..., :channels]
    imag_w = weight[..., channels:]
    lower = jnp.concatenate([-imag_w, real_w], axis=-1)
    return jnp.concatenate([weight, lower], axis=1)

def reference(fields, spectral_weight, local_weight):
    forward_lon = lon_forward_table(NLON, KX).astype(jnp.float32)
    backward_lon = lon_back_table(NLON, KX).astype(jnp.float32)
    forward_lat, backward_lat = lat_tables(NLAT, KY, ROWS_DEV)
    current = fields
    for layer_idx in range(LAYERS):
        wide = current.astype(jnp.float32)
        lon_modes = jnp.einsum('rcl,lpk->rkpc', wide, forward_lon)
        lon_modes = lon_modes.reshape(NLAT, KX, 2 * C).astype(jnp.bfloat16)
        lat_modes = lat_forward(forward_lat, lon_modes, C).astype(jnp.bfloat16)
        mixing = mix_matrix(spectral_weight[layer_idx], C).astype(jnp.float32)
        mixed_modes = jnp.einsum('jkc,kcd->jkd', lat_modes.astype(jnp.float32), mixing).astype(jnp.bfloat16)
        lat_back = lat_backward(backward_lat, mixed_modes, C).astype(jnp.bfloat16)
        spectral = jnp.einsum('rkpc,kpl->rcl', lat_back.reshape(NLAT, KX, 2, C).astype(jnp.float32), backward_lon)
        pointwise = jnp.einsum('rcl,cd->rdl', wide, local_weight[layer_idx].astype(jnp.float32))
        current = jax.nn.gelu(spectral + pointwise, approximate=True).astype(jnp.bfloat16)
    return current
```

```python
import functools
import math

import jax
import jax.numpy as jnp
import ml_dtypes
import numpy as np
from jax import lax
from jax.experimental import pallas as pl
from jax.experimental.pallas import tpu as pltpu
from jax.sharding import PartitionSpec as P

KY = 128
VMEM = 56 * 2**20
F32 = jnp.float32
BF16 = jnp.bfloat16


def rounded(table):
    return np.asarray(table, np.float32).astype(ml_dtypes.bfloat16)


def mode_order(mode_count, devices):
    per_device = mode_count // devices
    return np.arange(mode_count).reshape(devices, per_device).T.reshape(-1)


def lon_tables(lon_count, mode_count, devices):
    modes = mode_order(mode_count, devices).astype(np.int64)[:, None]
    cells = np.arange(lon_count, dtype=np.int64)[None, :]
    angle = 2.0 * np.pi / lon_count * (cells * modes % lon_count)
    both = np.concatenate([np.cos(angle), -np.sin(angle)], axis=0)
    return (rounded(both / math.sqrt(lon_count)), rounded(both / math.sqrt(mode_count)))


def lat_tables(lat_count, kept_count, block_rows):
    index = np.arange(kept_count, dtype=np.int64)
    waves = np.where(index < kept_count // 2, index, lat_count - kept_count + index)
    rowids = np.arange(lat_count, dtype=np.int64)
    latitudes = rowids % block_rows * (lat_count // block_rows) + rowids // block_rows
    angle = 2.0 * np.pi / lat_count * (waves[:, None] * latitudes[None, :] % lat_count)
    both = np.concatenate([np.cos(angle), np.sin(angle)], axis=0)
    return (rounded(both / math.sqrt(lat_count)), rounded(both.T / math.sqrt(kept_count)))


def low_half(shape, channels):
    return lax.broadcasted_iota(jnp.int32, shape, len(shape) - 1) % (2 * channels) < channels


def dot(a, b, dims):
    return lax.dot_general(a, b, (dims, ((), ())), preferred_element_type=F32)


def scatter_modes(modes_out, wide_ref, first_row, rows, block_rows, channels, devices):
    half = modes_out.shape[0] // 2
    per_device = half // devices
    lanes = 2 * channels
    low = low_half((half, lanes), channels)
    for pair in range(rows // 2):
        real = modes_out[:half, pair * lanes : (pair + 1) * lanes]
        imag = modes_out[half:, pair * lanes : (pair + 1) * lanes]
        even = jnp.where(low, real, pltpu.roll(imag, channels, 1))
        odd = jnp.where(low, pltpu.roll(real, channels, 1), imag)
        for offset, values in ((0, even), (1, odd)):
            row = first_row + 2 * pair + offset
            for k in range(per_device):
                wide_ref[k, pl.ds(row, devices, stride=block_rows), :] = values[
                    k * devices : (k + 1) * devices
                ]


def gather_modes(wide_ref, first_row, rows, block_rows, channels, devices):
    lanes = 2 * channels
    per_device = wide_ref.shape[0]
    low = low_half((per_device * devices, lanes), channels)
    reals, imags = [], []
    for pair in range(rows // 2):
        even, odd = [
            jnp.concatenate(
                [
                    wide_ref[
                        k, pl.ds(first_row + 2 * pair + offset, devices, stride=block_rows), :
                    ]
                    for k in range(per_device)
                ],
                axis=0,
            )
            for offset in range(2)
        ]
        reals.append(jnp.where(low, even, pltpu.roll(odd, channels, 1)))
        imags.append(jnp.where(low, pltpu.roll(even, channels, 1), odd))
    return jnp.concatenate(
        [jnp.concatenate(reals, axis=1), jnp.concatenate(imags, axis=1)], axis=0
    )


def pack(wide_ref, out_ref):
    lanes = wide_ref.shape[2]
    for k in range(wide_ref.shape[0]):
        out_ref[:, k * lanes : (k + 1) * lanes] = wide_ref[k].astype(BF16)


def unpack(in_ref, wide_ref):
    lanes = wide_ref.shape[2]
    for k in range(wide_ref.shape[0]):
        wide_ref[k] = in_ref[:, k * lanes : (k + 1) * lanes].astype(F32)


def wide_scratch(shape, channels):
    return pltpu.VMEM((shape[1] // (2 * channels), shape[0], 2 * channels), F32)


def first_kernel(block_rows, channels, devices, rows, fields_ref, table_ref, out_ref, wide_ref):
    step = pl.program_id(0)
    modes = dot(table_ref[...], fields_ref[...], ((1,), (1,)))
    scatter_modes(modes, wide_ref, step * rows, rows, block_rows, channels, devices)

    @pl.when(step == pl.num_programs(0) - 1)
    def _():
        pack(wide_ref, out_ref)


def first_transform(fields, table, block_rows, channels, devices, rows):
    lon_count = fields.shape[1]
    block = rows * channels
    wide = (devices * block_rows, table.shape[0] // devices * channels)
    return pl.pallas_call(
        functools.partial(first_kernel, block_rows, channels, devices, rows),
        grid=(block_rows // rows,),
        in_specs=[
            pl.BlockSpec((block, lon_count), lambda g: (g, 0)),
            pl.BlockSpec(table.shape, lambda g: (0, 0)),
        ],
        out_specs=pl.BlockSpec(wide, lambda g: (0, 0)),
        out_shape=jax.ShapeDtypeStruct(wide, BF16),
        scratch_shapes=[wide_scratch(wide, channels)],
        compiler_params=pltpu.CompilerParams(vmem_limit_bytes=VMEM),
    )(fields, table)


def middle_kernel(channels, values_ref, weight_ref, forward_ref, backward_ref, out_ref):
    kept = forward_ref.shape[0] // 2
    lanes = 2 * channels
    products = dot(forward_ref[...], values_ref[...], ((1,), (0,)))
    low = low_half((kept, lanes), channels)
    low_w = low_half((channels, lanes), channels)
    for k in range(values_ref.shape[1] // lanes):
        part = slice(k * lanes, (k + 1) * lanes)
        turned = pltpu.roll(products[kept:, part], channels, 1)
        modes = (products[:kept, part] + jnp.where(low, turned, -turned)).astype(BF16)
        weight = weight_ref[k].astype(F32)
        swapped = pltpu.roll(weight, channels, 1)
        mixing = jnp.concatenate([weight, jnp.where(low_w, -swapped, swapped)], axis=0)
        mixed = dot(modes, mixing.astype(BF16), ((1,), (0,)))
        swapped = pltpu.roll(mixed, channels, 1)
        both = jnp.concatenate([mixed, jnp.where(low, -swapped, swapped)], axis=0).astype(BF16)
        out_ref[:, part] = dot(backward_ref[...], both, ((1,), (0,))).astype(BF16)


def middle(values, weight, forward, backward, channels):
    return pl.pallas_call(
        functools.partial(middle_kernel, channels),
        out_shape=jax.ShapeDtypeStruct(values.shape, BF16),
        compiler_params=pltpu.CompilerParams(vmem_limit_bytes=VMEM),
    )(values, weight, forward, backward)


def gelu(x):
    u = x * (math.sqrt(2.0 / math.pi) + (0.044715 * math.sqrt(2.0 / math.pi)) * (x * x))
    half = 0.5 * x
    return half * jnp.tanh(u) + half


def back_kernel(
    block_rows, channels, devices, rows, again,
    modes_ref, field_ref, local_ref, back_ref, *rest,
):
    if again:
        table_ref, field_out_ref, modes_out_ref, wide_ref, wide_out_ref = rest
    else:
        field_out_ref, wide_ref = rest
    step = pl.program_id(0)

    @pl.when(step == 0)
    def _():
        unpack(modes_ref, wide_ref)

    modes = gather_modes(wide_ref, step * rows, rows, block_rows, channels, devices)
    modes = modes.T.astype(BF16)
    lhs = jnp.concatenate([modes, local_ref[...]], axis=1)
    lon_count = field_ref.shape[1]
    chunk = min(512, lon_count)
    total = None
    for start in range(0, lon_count, chunk):
        part = slice(start, start + chunk)
        rhs = jnp.concatenate([back_ref[:, part], field_ref[:, part]], axis=0)
        new = gelu(dot(lhs, rhs, ((1,), (0,)))).astype(BF16)
        field_out_ref[:, part] = new
        if again:
            product = dot(table_ref[:, part], new, ((1,), (1,)))
            total = product if total is None else total + product
    if again:
        scatter_modes(total, wide_out_ref, step * rows, rows, block_rows, channels, devices)

        @pl.when(step == pl.num_programs(0) - 1)
        def _():
            pack(wide_out_ref, modes_out_ref)


def back_transform(modes, field, local, back, table, block_rows, channels, devices, rows):
    again = table is not None
    block = rows * channels
    lon_count = field.shape[1]
    whole = lambda array: pl.BlockSpec(array.shape, lambda g: (0, 0))
    field_spec = pl.BlockSpec((block, lon_count), lambda g: (g, 0))
    args = [modes, field, local, back] + ([table] if again else [])
    out_specs, out_shape = [field_spec], [jax.ShapeDtypeStruct(field.shape, BF16)]
    scratch = [wide_scratch(modes.shape, channels)]
    if again:
        out_specs.append(whole(modes))
        out_shape.append(jax.ShapeDtypeStruct(modes.shape, BF16))
        scratch.append(wide_scratch(modes.shape, channels))
    return pl.pallas_call(
        functools.partial(back_kernel, block_rows, channels, devices, rows, again),
        grid=(block_rows // rows,),
        in_specs=[whole(modes), field_spec, whole(local), whole(back)]
        + ([whole(table)] if again else []),
        out_specs=out_specs,
        out_shape=out_shape,
        scratch_shapes=scratch,
        compiler_params=pltpu.CompilerParams(vmem_limit_bytes=VMEM),
    )(*args)


def exchange(array, devices):
    parts = array.reshape(devices, array.shape[0] // devices, array.shape[1])
    return lax.all_to_all(parts, "lat", 0, 0, tiled=True).reshape(array.shape)


def shards(fields, spectral_weight, local_weight):
    block_rows, channels, lon_count = fields.shape
    layer_count, mode_count = spectral_weight.shape[:2]
    devices = lax.axis_size("lat")
    rows = max(2, 256 // channels)
    per_device = mode_count // devices
    forward_lon, backward_lon = lon_tables(lon_count, mode_count, devices)
    forward_lat, backward_lat = lat_tables(block_rows * devices, KY, block_rows)
    own = lax.dynamic_slice_in_dim(
        spectral_weight, lax.axis_index("lat") * per_device, per_device, 1
    )
    mixers = jnp.einsum(
        "rs,lcd->lrdsc", jnp.eye(rows, dtype=BF16), local_weight
    ).reshape(layer_count, rows * channels, rows * channels)
    sizes = (block_rows, channels, devices, rows)
    current = fields.reshape(block_rows * channels, lon_count)
    modes = first_transform(current, forward_lon, *sizes)
    for layer in range(layer_count):
        arrived = exchange(modes, devices)
        rebuilt = middle(arrived, own[layer], forward_lat, backward_lat, channels)
        returned = exchange(rebuilt, devices)
        last = layer == layer_count - 1
        result = back_transform(
            returned, current, mixers[layer], backward_lon, None if last else forward_lon, *sizes
        )
        current, modes = (result[0], None) if last else result
    return current.reshape(fields.shape)


def solution(mesh):
    return jax.shard_map(
        shards,
        mesh=mesh,
        in_specs=(P(("grp", "lat"), None, None), P(), P()),
        out_specs=P(("grp", "lat"), None, None),
        check_vma=False,
    )
```

```python
import functools
import math

import jax
import jax.numpy as jnp
import ml_dtypes
import numpy as np
from jax import lax
from jax.experimental import pallas as pl
from jax.experimental.pallas import tpu as pltpu
from jax.sharding import PartitionSpec as P

KY = 128
F32 = jnp.float32
BF16 = jnp.bfloat16


def rounded(table):
    return np.asarray(table, np.float32).astype(ml_dtypes.bfloat16)


def mode_order(mode_count, devices):
    per_device = mode_count // devices
    return np.arange(mode_count).reshape(devices, per_device).T.reshape(-1)


def lon_tables(lon_count, mode_count, devices):
    modes = mode_order(mode_count, devices).astype(np.int64)[:, None]
    cells = np.arange(lon_count, dtype=np.int64)[None, :]
    angle = 2.0 * np.pi / lon_count * (cells * modes % lon_count)
    both = np.concatenate([np.cos(angle), -np.sin(angle)], axis=0)
    return (rounded(both / math.sqrt(lon_count)), rounded(both / math.sqrt(mode_count)))


def lat_tables(lat_count, kept_count, block_rows):
    index = np.arange(kept_count, dtype=np.int64)
    waves = np.where(index < kept_count // 2, index, lat_count - kept_count + index)
    rowids = np.arange(lat_count, dtype=np.int64)
    latitudes = rowids % block_rows * (lat_count // block_rows) + rowids // block_rows
    angle = 2.0 * np.pi / lat_count * (waves[:, None] * latitudes[None, :] % lat_count)
    both = np.concatenate([np.cos(angle), np.sin(angle)], axis=0)
    return (rounded(both / math.sqrt(lat_count)), rounded(both.T / math.sqrt(kept_count)))


def low_half(shape, channels):
    return lax.broadcasted_iota(jnp.int32, shape, len(shape) - 1) % (2 * channels) < channels


def dot(a, b, dims):
    return lax.dot_general(a, b, (dims, ((), ())), preferred_element_type=F32)


def scatter_modes(modes_out, wide_ref, first_row, rows, block_rows, channels, devices):
    half = modes_out.shape[0] // 2
    per_device = half // devices
    lanes = 2 * channels
    low = low_half((half, lanes), channels)
    for pair in range(rows // 2):
        real = modes_out[:half, pair * lanes : (pair + 1) * lanes]
        imag = modes_out[half:, pair * lanes : (pair + 1) * lanes]
        even = jnp.where(low, real, pltpu.roll(imag, channels, 1))
        odd = jnp.where(low, pltpu.roll(real, channels, 1), imag)
        for offset, values in ((0, even), (1, odd)):
            row = first_row + 2 * pair + offset
            for k in range(per_device):
                wide_ref[k, pl.ds(row, devices, stride=block_rows), :] = values[
                    k * devices : (k + 1) * devices
                ]


def gather_modes(wide_ref, first_row, rows, block_rows, channels, devices):
    lanes = 2 * channels
    per_device = wide_ref.shape[0]
    low = low_half((per_device * devices, lanes), channels)
    reals, imags = [], []
    for pair in range(rows // 2):
        even, odd = [
            jnp.concatenate(
                [
                    wide_ref[
                        k, pl.ds(first_row + 2 * pair + offset, devices, stride=block_rows), :
                    ]
                    for k in range(per_device)
                ],
                axis=0,
            )
            for offset in range(2)
        ]
        reals.append(jnp.where(low, even, pltpu.roll(odd, channels, 1)))
        imags.append(jnp.where(low, pltpu.roll(even, channels, 1), odd))
    return jnp.concatenate(
        [jnp.concatenate(reals, axis=1), jnp.concatenate(imags, axis=1)], axis=0
    )


def pack(wide_ref, out_ref):
    lanes = wide_ref.shape[2]
    for k in range(wide_ref.shape[0]):
        out_ref[:, k * lanes : (k + 1) * lanes] = wide_ref[k].astype(BF16)


def unpack(in_ref, wide_ref):
    lanes = wide_ref.shape[2]
    for k in range(wide_ref.shape[0]):
        wide_ref[k] = in_ref[:, k * lanes : (k + 1) * lanes].astype(F32)


def wide_scratch(shape, channels):
    return pltpu.VMEM((shape[1] // (2 * channels), shape[0], 2 * channels), F32)


def in_vmem(array):
    return pltpu.with_memory_space_constraint(array, pltpu.VMEM)


def in_hbm(array):
    return pltpu.with_memory_space_constraint(array, pltpu.HBM)


def params(limit):
    return pltpu.CompilerParams(vmem_limit_bytes=limit * 2**20)


OUTSIDE = pl.BlockSpec(memory_space=pltpu.HBM)
RESIDENT = pl.BlockSpec(memory_space=pltpu.VMEM)


def first_kernel(
    block_rows, channels, devices, rows,
    fields_ref, table_ref, modes_ref, copy_ref, table_copy, wide_ref, sems,
):
    steps, block = block_rows // rows, rows * channels
    copies = [pltpu.make_async_copy(table_ref, table_copy, sems.at[steps])]
    for step in range(steps):
        part = pl.ds(step * block, block)
        copies.append(
            pltpu.make_async_copy(fields_ref.at[part], copy_ref.at[part], sems.at[step])
        )
    for copy in copies:
        copy.start()
    copies[0].wait()
    for step in range(steps):
        copies[step + 1].wait()
        part = slice(step * block, (step + 1) * block)
        modes = dot(table_copy[...], copy_ref[part, :], ((1,), (1,)))
        scatter_modes(modes, wide_ref, step * rows, rows, block_rows, channels, devices)
    pack(wide_ref, modes_ref)


def first_transform(fields, table, block_rows, channels, devices, rows):
    modes_shape = (devices * block_rows, table.shape[0] // devices * channels)
    return pl.pallas_call(
        functools.partial(first_kernel, block_rows, channels, devices, rows),
        in_specs=[OUTSIDE, OUTSIDE],
        out_specs=RESIDENT,
        out_shape=pltpu.VMEM(modes_shape, BF16),
        scratch_shapes=[
            pltpu.VMEM(fields.shape, BF16),
            pltpu.VMEM(table.shape, BF16),
            wide_scratch(modes_shape, channels),
            pltpu.SemaphoreType.DMA((block_rows // rows + 1,)),
        ],
        compiler_params=params(24),
    )(in_hbm(fields), in_hbm(table))


def local_kernel(field_ref, weight_ref, out_ref):
    out_ref[...] = dot(weight_ref[...], field_ref[...], ((1,), (0,))).astype(BF16)


def local_mix(field, weight):
    block = pl.BlockSpec((weight.shape[0], field.shape[1]), lambda g: (g, 0))
    return pl.pallas_call(
        local_kernel,
        grid=(field.shape[0] // weight.shape[0],),
        in_specs=[block, pl.BlockSpec(weight.shape, lambda g: (0, 0))],
        out_specs=block,
        out_shape=pltpu.HBM(field.shape, BF16),
        compiler_params=params(16),
    )(in_hbm(field), weight)


def middle_kernel(channels, values_ref, weight_ref, forward_ref, backward_ref, out_ref):
    kept = forward_ref.shape[0] // 2
    lanes = 2 * channels
    products = dot(forward_ref[...], values_ref[...], ((1,), (0,)))
    low = low_half((kept, lanes), channels)
    low_w = low_half((channels, lanes), channels)
    for k in range(values_ref.shape[1] // lanes):
        part = slice(k * lanes, (k + 1) * lanes)
        turned = pltpu.roll(products[kept:, part], channels, 1)
        modes = (products[:kept, part] + jnp.where(low, turned, -turned)).astype(BF16)
        weight = weight_ref[k].astype(F32)
        swapped = pltpu.roll(weight, channels, 1)
        mixing = jnp.concatenate([weight, jnp.where(low_w, -swapped, swapped)], axis=0)
        mixed = dot(modes, mixing.astype(BF16), ((1,), (0,)))
        swapped = pltpu.roll(mixed, channels, 1)
        both = jnp.concatenate([mixed, jnp.where(low, -swapped, swapped)], axis=0).astype(BF16)
        out_ref[:, part] = dot(backward_ref[...], both, ((1,), (0,))).astype(BF16)


def middle(values, weight, forward, backward, channels):
    return pl.pallas_call(
        functools.partial(middle_kernel, channels),
        in_specs=[RESIDENT] * 4,
        out_specs=RESIDENT,
        out_shape=pltpu.VMEM(values.shape, BF16),
        compiler_params=params(24),
    )(in_vmem(values), in_vmem(weight), in_vmem(forward), in_vmem(backward))


def gelu(x):
    u = x * (math.sqrt(2.0 / math.pi) + (0.044715 * math.sqrt(2.0 / math.pi)) * (x * x))
    half = 0.5 * x
    return half * jnp.tanh(u) + half


def spectral_block(modes, local_ref, back_ref, out_ref, first):
    lon_count = back_ref.shape[1]
    chunk = min(256, lon_count)
    for start in range(0, lon_count, chunk):
        place = (slice(first, first + modes.shape[0]), slice(start, start + chunk))
        total = dot(modes, back_ref[:, place[1]], ((1,), (0,))) + local_ref[place].astype(F32)
        out_ref[place] = gelu(total).astype(BF16)


def row_copies(source_ref, target_ref, sems, steps):
    block = source_ref.shape[0] // steps
    parts = [pl.ds(step * block, block) for step in range(steps)]
    return [
        pltpu.make_async_copy(source_ref.at[part], target_ref.at[part], sems.at[step])
        for step, part in enumerate(parts)
    ]


def back_kernel(block_rows, channels, devices, rows, again, modes_ref, local_ref, back_ref, *rest):
    if again:
        table_ref, field_out_ref, modes_out_ref = rest[:3]
        wide_out_ref = rest[-1]
        rest = rest[3:-1]
    else:
        field_out_ref = rest[0]
        rest = rest[1:]
    local_copy, field_ref, wide_ref, in_sems, out_sems = rest
    steps, block = block_rows // rows, rows * channels
    arriving = row_copies(local_ref, local_copy, in_sems, steps)
    leaving = row_copies(field_ref, field_out_ref, out_sems, steps)
    for copy in arriving:
        copy.start()
    unpack(modes_ref, wide_ref)
    for step in range(steps):
        modes = gather_modes(wide_ref, step * rows, rows, block_rows, channels, devices)
        arriving[step].wait()
        spectral_block(modes.T.astype(BF16), local_copy, back_ref, field_ref, step * block)
        leaving[step].start()
        if again:
            field = field_ref[step * block : (step + 1) * block, :]
            product = dot(table_ref[...], field, ((1,), (1,)))
            scatter_modes(product, wide_out_ref, step * rows, rows, block_rows, channels, devices)
    if again:
        pack(wide_out_ref, modes_out_ref)
    for copy in leaving:
        copy.wait()


def back_transform(modes, local, back, table, block_rows, channels, devices, rows):
    again = table is not None
    steps = block_rows // rows
    scratch = [
        pltpu.VMEM(local.shape, BF16),
        pltpu.VMEM(local.shape, BF16),
        wide_scratch(modes.shape, channels),
        pltpu.SemaphoreType.DMA((steps,)),
        pltpu.SemaphoreType.DMA((steps,)),
    ]
    args = [in_vmem(modes), in_hbm(local), in_vmem(back)]
    out_shape = [pltpu.HBM(local.shape, BF16)]
    if again:
        args.append(in_vmem(table))
        out_shape.append(pltpu.VMEM(modes.shape, BF16))
        scratch.append(wide_scratch(modes.shape, channels))
    return pl.pallas_call(
        functools.partial(back_kernel, block_rows, channels, devices, rows, again),
        in_specs=[RESIDENT, OUTSIDE] + [RESIDENT] * (len(args) - 2),
        out_specs=[OUTSIDE] + [RESIDENT] * (len(out_shape) - 1),
        out_shape=out_shape,
        scratch_shapes=scratch,
        compiler_params=params(32),
    )(*args)


def exchange(array, devices):
    parts = array.reshape(devices, array.shape[0] // devices, array.shape[1])
    return lax.all_to_all(parts, "lat", 0, 0, tiled=True).reshape(array.shape)


def shards(fields, spectral_weight, local_weight):
    block_rows, channels, lon_count = fields.shape
    layer_count, mode_count = spectral_weight.shape[:2]
    devices = lax.axis_size("lat")
    rows = max(2, 256 // channels)
    per_device = mode_count // devices
    forward_lon, backward_lon = lon_tables(lon_count, mode_count, devices)
    forward_lat, backward_lat = lat_tables(block_rows * devices, KY, block_rows)
    own = lax.dynamic_slice_in_dim(
        spectral_weight, lax.axis_index("lat") * per_device, per_device, 1
    )
    mixers = jnp.einsum(
        "rs,lcd->lrdsc", jnp.eye(rows, dtype=BF16), local_weight
    ).reshape(layer_count, rows * channels, rows * channels)
    wide_rows = 2 * rows if block_rows % (2 * rows) == 0 else rows
    sizes = (block_rows, channels, devices)
    field = fields.reshape(block_rows * channels, lon_count)
    modes = first_transform(field, forward_lon, *sizes, rows)
    for layer in range(layer_count):
        arrived = exchange(modes, devices)
        rebuilt = middle(arrived, own[layer], forward_lat, backward_lat, channels)
        returned = exchange(rebuilt, devices)
        local = local_mix(field, mixers[layer])
        if layer < layer_count - 1:
            field, modes = back_transform(
                returned, local, backward_lon, forward_lon, *sizes, wide_rows
            )
        else:
            field = back_transform(returned, local, backward_lon, None, *sizes, rows)[0]
    return field.reshape(fields.shape)


def solution(mesh):
    return jax.shard_map(
        shards,
        mesh=mesh,
        in_specs=(P(("grp", "lat"), None, None), P(), P()),
        out_specs=P(("grp", "lat"), None, None),
        check_vma=False,
    )
```

```python
import functools
import math

import jax
import jax.numpy as jnp
import ml_dtypes
import numpy as np
from jax import lax
from jax.experimental import pallas as pl
from jax.experimental.pallas import tpu as pltpu
from jax.sharding import PartitionSpec as P

KY = 128
F32 = jnp.float32
BF16 = jnp.bfloat16


def rounded(table):
    return np.asarray(table, np.float32).astype(ml_dtypes.bfloat16)


def mode_order(mode_count, devices):
    per_device = mode_count // devices
    return np.arange(mode_count).reshape(devices, per_device).T.reshape(-1)


def lon_tables(lon_count, mode_count, devices):
    modes = mode_order(mode_count, devices).astype(np.int64)[:, None]
    cells = np.arange(lon_count, dtype=np.int64)[None, :]
    angle = 2.0 * np.pi / lon_count * (cells * modes % lon_count)
    both = np.concatenate([np.cos(angle), -np.sin(angle)], axis=0)
    return (rounded(both / math.sqrt(lon_count)), rounded(both / math.sqrt(mode_count) * 0.5))


def lat_tables(lat_count, kept_count, block_rows):
    index = np.arange(kept_count, dtype=np.int64)
    waves = np.where(index < kept_count // 2, index, lat_count - kept_count + index)
    rowids = np.arange(lat_count, dtype=np.int64)
    latitudes = rowids % block_rows * (lat_count // block_rows) + rowids // block_rows
    angle = 2.0 * np.pi / lat_count * (waves[:, None] * latitudes[None, :] % lat_count)
    both = np.concatenate([np.cos(angle), np.sin(angle)], axis=0)
    return (rounded(both / math.sqrt(lat_count)), rounded(both.T / math.sqrt(kept_count)))


def low_half(shape, channels):
    return lax.broadcasted_iota(jnp.int32, shape, len(shape) - 1) % (2 * channels) < channels


def dot(a, b, dims):
    return lax.dot_general(a, b, (dims, ((), ())), preferred_element_type=F32)


def scatter_modes(modes_out, wide_ref, first_row, rows, block_rows, channels, devices):
    half = modes_out.shape[0] // 2
    per_device = half // devices
    lanes = 2 * channels
    low = low_half((half, lanes), channels)
    for pair in range(rows // 2):
        real = modes_out[:half, pair * lanes : (pair + 1) * lanes]
        imag = modes_out[half:, pair * lanes : (pair + 1) * lanes]
        even = jnp.where(low, real, pltpu.roll(imag, channels, 1))
        odd = jnp.where(low, pltpu.roll(real, channels, 1), imag)
        for offset, values in ((0, even), (1, odd)):
            row = first_row + 2 * pair + offset
            for k in range(per_device):
                wide_ref[k, pl.ds(row, devices, stride=block_rows), :] = values[
                    k * devices : (k + 1) * devices
                ]


def gather_modes(wide_ref, first_row, rows, block_rows, channels, devices):
    lanes = 2 * channels
    per_device = wide_ref.shape[0]
    low = low_half((per_device * devices, lanes), channels)
    reals, imags = [], []
    for pair in range(rows // 2):
        even, odd = [
            jnp.concatenate(
                [
                    wide_ref[
                        k, pl.ds(first_row + 2 * pair + offset, devices, stride=block_rows), :
                    ]
                    for k in range(per_device)
                ],
                axis=0,
            )
            for offset in range(2)
        ]
        reals.append(jnp.where(low, even, pltpu.roll(odd, channels, 1)))
        imags.append(jnp.where(low, pltpu.roll(even, channels, 1), odd))
    return jnp.concatenate(
        [jnp.concatenate(reals, axis=1), jnp.concatenate(imags, axis=1)], axis=0
    )


def pack(wide_ref, out_ref):
    lanes = wide_ref.shape[2]
    for k in range(wide_ref.shape[0]):
        out_ref[:, k * lanes : (k + 1) * lanes] = wide_ref[k].astype(BF16)


def unpack(in_ref, wide_ref):
    lanes = wide_ref.shape[2]
    for k in range(wide_ref.shape[0]):
        wide_ref[k] = in_ref[:, k * lanes : (k + 1) * lanes].astype(F32)


def wide_scratch(shape, channels):
    return pltpu.VMEM((shape[1] // (2 * channels), shape[0], 2 * channels), F32)


def in_vmem(array):
    return pltpu.with_memory_space_constraint(array, pltpu.VMEM)


def in_hbm(array):
    return pltpu.with_memory_space_constraint(array, pltpu.HBM)


def params(limit):
    return pltpu.CompilerParams(vmem_limit_bytes=limit * 2**20)


OUTSIDE = pl.BlockSpec(memory_space=pltpu.HBM)
RESIDENT = pl.BlockSpec(memory_space=pltpu.VMEM)


def first_kernel(
    block_rows, channels, devices, rows,
    fields_ref, table_ref, modes_ref, copy_ref, table_copy, wide_ref, sems,
):
    steps, block = block_rows // rows, rows * channels
    table_read = pltpu.make_async_copy(table_ref, table_copy, sems.at[steps])

    def read(step):
        part = pl.ds(step * block, block)
        return pltpu.make_async_copy(fields_ref.at[part], copy_ref.at[part], sems.at[step])

    table_read.start()
    for step in range(steps):
        read(step).start()
    table_read.wait()

    def body(step, carry):
        read(step).wait()
        field = copy_ref[pl.ds(pl.multiple_of(step * block, block), block), :]
        modes = dot(table_copy[...], field, ((1,), (1,)))
        scatter_modes(modes, wide_ref, step * rows, rows, block_rows, channels, devices)
        return carry

    lax.fori_loop(0, steps, body, 0)
    pack(wide_ref, modes_ref)


def first_transform(fields, table, block_rows, channels, devices, rows):
    modes_shape = (devices * block_rows, table.shape[0] // devices * channels)
    return pl.pallas_call(
        functools.partial(first_kernel, block_rows, channels, devices, rows),
        in_specs=[OUTSIDE, OUTSIDE],
        out_specs=RESIDENT,
        out_shape=pltpu.VMEM(modes_shape, BF16),
        scratch_shapes=[
            pltpu.VMEM(fields.shape, BF16),
            pltpu.VMEM(table.shape, BF16),
            wide_scratch(modes_shape, channels),
            pltpu.SemaphoreType.DMA((block_rows // rows + 1,)),
        ],
        compiler_params=params(24),
    )(in_hbm(fields), in_hbm(table))


def local_kernel(field_ref, weight_ref, out_ref):
    out_ref[...] = dot(weight_ref[...], field_ref[...], ((1,), (0,))).astype(BF16)


def local_mix(field, weight):
    block = pl.BlockSpec((weight.shape[0], field.shape[1]), lambda g: (g, 0))
    return pl.pallas_call(
        local_kernel,
        grid=(field.shape[0] // weight.shape[0],),
        in_specs=[block, pl.BlockSpec(weight.shape, lambda g: (0, 0))],
        out_specs=block,
        out_shape=pltpu.HBM(field.shape, BF16),
        compiler_params=params(16),
    )(in_hbm(field), weight)


def middle_kernel(channels, values_ref, weight_ref, forward_ref, backward_ref, out_ref):
    kept = forward_ref.shape[0] // 2
    lanes = 2 * channels
    products = dot(forward_ref[...], values_ref[...], ((1,), (0,)))
    low = low_half((kept, lanes), channels)
    low_w = low_half((channels, lanes), channels)
    for k in range(values_ref.shape[1] // lanes):
        part = slice(k * lanes, (k + 1) * lanes)
        turned = pltpu.roll(products[kept:, part], channels, 1)
        modes = (products[:kept, part] + jnp.where(low, turned, -turned)).astype(BF16)
        weight = weight_ref[k].astype(F32)
        swapped = pltpu.roll(weight, channels, 1)
        mixing = jnp.concatenate([weight, jnp.where(low_w, -swapped, swapped)], axis=0)
        mixed = dot(modes, mixing.astype(BF16), ((1,), (0,)))
        swapped = pltpu.roll(mixed, channels, 1)
        both = jnp.concatenate([mixed, jnp.where(low, -swapped, swapped)], axis=0).astype(BF16)
        out_ref[:, part] = dot(backward_ref[...], both, ((1,), (0,))).astype(BF16)


def middle(values, weight, forward, backward, channels):
    return pl.pallas_call(
        functools.partial(middle_kernel, channels),
        in_specs=[RESIDENT] * 4,
        out_specs=RESIDENT,
        out_shape=pltpu.VMEM(values.shape, BF16),
        compiler_params=params(24),
    )(in_vmem(values), in_vmem(weight), in_vmem(forward), in_vmem(backward))


def gelu_of_double(v):
    scale = math.sqrt(2.0 / math.pi)
    return v * jnp.tanh(v * (BF16(2.0 * scale) + BF16(8.0 * 0.044715 * scale) * (v * v))) + v


def spectral_block(modes, back_ref, local_ref, out_ref, first):
    lon_count = back_ref.shape[1]
    chunk = min(256, lon_count)
    rows = slice(first, first + modes.shape[0])
    for start in range(0, lon_count, chunk):
        part = slice(start, start + chunk)
        total = dot(modes, back_ref[:, part], ((1,), (0,))) + local_ref[rows, part].astype(F32)
        local_ref[rows, part] = total.astype(BF16)
    out_ref[rows, :] = gelu_of_double(local_ref[rows, :])


def row_copies(source_ref, target_ref, sems, steps):
    block = source_ref.shape[0] // steps
    parts = [pl.ds(step * block, block) for step in range(steps)]
    return [
        pltpu.make_async_copy(source_ref.at[part], target_ref.at[part], sems.at[step])
        for step, part in enumerate(parts)
    ]


def back_kernel(block_rows, channels, devices, rows, again, modes_ref, local_ref, back_ref, *rest):
    if again:
        table_ref, field_out_ref, modes_out_ref = rest[:3]
        wide_out_ref = rest[-1]
        rest = rest[3:-1]
    else:
        field_out_ref = rest[0]
        rest = rest[1:]
    local_copy, field_ref, wide_ref, lhs_ref, in_sems, out_sems = rest
    steps, block = block_rows // rows, rows * channels
    arriving = row_copies(local_ref, local_copy, in_sems, steps)
    leaving = row_copies(field_ref, field_out_ref, out_sems, steps)
    for copy in arriving:
        copy.start()
    unpack(modes_ref, wide_ref)
    for step in range(steps):
        modes = gather_modes(wide_ref, step * rows, rows, block_rows, channels, devices)
        lhs_ref[step * block : (step + 1) * block, :] = modes.T.astype(BF16)
    for step in range(steps):
        part = slice(step * block, (step + 1) * block)
        arriving[step].wait()
        spectral_block(lhs_ref[part, :], back_ref, local_copy, field_ref, step * block)
        leaving[step].start()
        if again:
            product = dot(table_ref[...], field_ref[part, :], ((1,), (1,)))
            scatter_modes(product, wide_out_ref, step * rows, rows, block_rows, channels, devices)
    if again:
        pack(wide_out_ref, modes_out_ref)
    for copy in leaving:
        copy.wait()


def back_transform(modes, local, back, table, block_rows, channels, devices, rows):
    again = table is not None
    steps = block_rows // rows
    scratch = [
        pltpu.VMEM(local.shape, BF16),
        pltpu.VMEM(local.shape, BF16),
        wide_scratch(modes.shape, channels),
        pltpu.VMEM((local.shape[0], back.shape[0]), BF16),
        pltpu.SemaphoreType.DMA((steps,)),
        pltpu.SemaphoreType.DMA((steps,)),
    ]
    args = [in_vmem(modes), in_hbm(local), in_vmem(back)]
    out_shape = [pltpu.HBM(local.shape, BF16)]
    if again:
        args.append(in_vmem(table))
        out_shape.append(pltpu.VMEM(modes.shape, BF16))
        scratch.append(wide_scratch(modes.shape, channels))
    return pl.pallas_call(
        functools.partial(back_kernel, block_rows, channels, devices, rows, again),
        in_specs=[RESIDENT, OUTSIDE] + [RESIDENT] * (len(args) - 2),
        out_specs=[OUTSIDE] + [RESIDENT] * (len(out_shape) - 1),
        out_shape=out_shape,
        scratch_shapes=scratch,
        compiler_params=params(32),
    )(*args)


def exchange(array, devices):
    parts = array.reshape(devices, array.shape[0] // devices, array.shape[1])
    return lax.all_to_all(parts, "lat", 0, 0, tiled=True).reshape(array.shape)


def shards(fields, spectral_weight, local_weight):
    block_rows, channels, lon_count = fields.shape
    layer_count, mode_count = spectral_weight.shape[:2]
    devices = lax.axis_size("lat")
    rows = max(2, 256 // channels)
    per_device = mode_count // devices
    forward_lon, backward_lon = lon_tables(lon_count, mode_count, devices)
    forward_lat, backward_lat = lat_tables(block_rows * devices, KY, block_rows)
    own = lax.dynamic_slice_in_dim(
        spectral_weight, lax.axis_index("lat") * per_device, per_device, 1
    )
    mixers = jnp.einsum(
        "rs,lcd->lrdsc", 0.5 * jnp.eye(rows, dtype=BF16), local_weight
    ).reshape(layer_count, rows * channels, rows * channels)
    wide_rows = 2 * rows if block_rows % (2 * rows) == 0 else rows
    sizes = (block_rows, channels, devices)
    field = fields.reshape(block_rows * channels, lon_count)
    modes = first_transform(field, forward_lon, *sizes, wide_rows)
    for layer in range(layer_count):
        arrived = exchange(modes, devices)
        rebuilt = middle(arrived, own[layer], forward_lat, backward_lat, channels)
        returned = exchange(rebuilt, devices)
        local = local_mix(field, mixers[layer])
        if layer < layer_count - 1:
            field, modes = back_transform(
                returned, local, backward_lon, forward_lon, *sizes, wide_rows
            )
        else:
            field = back_transform(returned, local, backward_lon, None, *sizes, wide_rows)[0]
    return field.reshape(fields.shape)


def solution(mesh):
    return jax.shard_map(
        shards,
        mesh=mesh,
        in_specs=(P(("grp", "lat"), None, None), P(), P()),
        out_specs=P(("grp", "lat"), None, None),
        check_vma=False,
    )
```

```python
import functools
import math

import jax
import jax.numpy as jnp
import ml_dtypes
import numpy as np
from jax import lax
from jax.experimental import pallas as pl
from jax.experimental.pallas import tpu as pltpu
from jax.sharding import PartitionSpec as P

KY = 128
F32 = jnp.float32
BF16 = jnp.bfloat16


def rounded(table):
    return np.asarray(table, np.float32).astype(ml_dtypes.bfloat16)


def mode_order(mode_count, devices):
    per_device = mode_count // devices
    return np.arange(mode_count).reshape(devices, per_device).T.reshape(-1)


def lon_tables(lon_count, mode_count, devices):
    modes = mode_order(mode_count, devices).astype(np.int64)[:, None]
    cells = np.arange(lon_count, dtype=np.int64)[None, :]
    angle = 2.0 * np.pi / lon_count * (cells * modes % lon_count)
    both = np.concatenate([np.cos(angle), -np.sin(angle)], axis=0)
    return (rounded(both / math.sqrt(lon_count)), rounded(both / math.sqrt(mode_count) * 0.5))


def lat_tables(lat_count, kept_count, block_rows):
    index = np.arange(kept_count, dtype=np.int64)
    waves = np.where(index < kept_count // 2, index, lat_count - kept_count + index)
    rowids = np.arange(lat_count, dtype=np.int64)
    latitudes = rowids % block_rows * (lat_count // block_rows) + rowids // block_rows
    angle = 2.0 * np.pi / lat_count * (waves[:, None] * latitudes[None, :] % lat_count)
    both = np.concatenate([np.cos(angle), np.sin(angle)], axis=0)
    return (rounded(both / math.sqrt(lat_count)), rounded(both.T / math.sqrt(kept_count)))


def low_half(shape, channels):
    return lax.broadcasted_iota(jnp.int32, shape, len(shape) - 1) % (2 * channels) < channels


def dot(a, b, dims):
    return lax.dot_general(a, b, (dims, ((), ())), preferred_element_type=F32)


def scatter_modes(modes_out, wide_ref, first_row, rows, block_rows, channels, devices):
    half = modes_out.shape[0] // 2
    per_device = half // devices
    lanes = 2 * channels
    low = low_half((half, lanes), channels)
    for pair in range(rows // 2):
        real = modes_out[:half, pair * lanes : (pair + 1) * lanes]
        imag = modes_out[half:, pair * lanes : (pair + 1) * lanes]
        even = jnp.where(low, real, pltpu.roll(imag, channels, 1))
        odd = jnp.where(low, pltpu.roll(real, channels, 1), imag)
        for offset, values in ((0, even), (1, odd)):
            row = first_row + 2 * pair + offset
            for k in range(per_device):
                wide_ref[k, pl.ds(row, devices, stride=block_rows), :] = values[
                    k * devices : (k + 1) * devices
                ]


def gather_modes(wide_ref, first_row, rows, block_rows, channels, devices):
    lanes = 2 * channels
    per_device = wide_ref.shape[0]
    low = low_half((per_device * devices, lanes), channels)
    reals, imags = [], []
    for pair in range(rows // 2):
        even, odd = [
            jnp.concatenate(
                [
                    wide_ref[
                        k, pl.ds(first_row + 2 * pair + offset, devices, stride=block_rows), :
                    ]
                    for k in range(per_device)
                ],
                axis=0,
            )
            for offset in range(2)
        ]
        reals.append(jnp.where(low, even, pltpu.roll(odd, channels, 1)))
        imags.append(jnp.where(low, pltpu.roll(even, channels, 1), odd))
    return jnp.concatenate(
        [jnp.concatenate(reals, axis=1), jnp.concatenate(imags, axis=1)], axis=0
    )


def pack(wide_ref, out_ref):
    lanes = wide_ref.shape[2]
    for k in range(wide_ref.shape[0]):
        out_ref[:, k * lanes : (k + 1) * lanes] = wide_ref[k].astype(BF16)


def unpack(in_ref, wide_ref):
    lanes = wide_ref.shape[2]
    for k in range(wide_ref.shape[0]):
        wide_ref[k] = in_ref[:, k * lanes : (k + 1) * lanes].astype(F32)


def wide_scratch(shape, channels):
    return pltpu.VMEM((shape[1] // (2 * channels), shape[0], 2 * channels), F32)


def in_vmem(array):
    return pltpu.with_memory_space_constraint(array, pltpu.VMEM)


def in_hbm(array):
    return pltpu.with_memory_space_constraint(array, pltpu.HBM)


def params(limit):
    return pltpu.CompilerParams(vmem_limit_bytes=limit * 2**20)


OUTSIDE = pl.BlockSpec(memory_space=pltpu.HBM)
RESIDENT = pl.BlockSpec(memory_space=pltpu.VMEM)


def first_kernel(
    block_rows, channels, devices, rows,
    fields_ref, table_ref, modes_ref, copy_ref, table_copy, wide_ref, sems,
):
    steps, block = block_rows // rows, rows * channels
    table_read = pltpu.make_async_copy(table_ref, table_copy, sems.at[steps])

    def read(step):
        part = pl.ds(step * block, block)
        return pltpu.make_async_copy(fields_ref.at[part], copy_ref.at[part], sems.at[step])

    table_read.start()
    for step in range(steps):
        read(step).start()
    table_read.wait()

    def body(step, carry):
        read(step).wait()
        field = copy_ref[pl.ds(pl.multiple_of(step * block, block), block), :]
        modes = dot(table_copy[...], field, ((1,), (1,)))
        scatter_modes(modes, wide_ref, step * rows, rows, block_rows, channels, devices)
        return carry

    lax.fori_loop(0, steps, body, 0)
    pack(wide_ref, modes_ref)


def first_transform(fields, table, block_rows, channels, devices, rows):
    modes_shape = (devices * block_rows, table.shape[0] // devices * channels)
    return pl.pallas_call(
        functools.partial(first_kernel, block_rows, channels, devices, rows),
        in_specs=[OUTSIDE, OUTSIDE],
        out_specs=RESIDENT,
        out_shape=pltpu.VMEM(modes_shape, BF16),
        scratch_shapes=[
            pltpu.VMEM(fields.shape, BF16),
            pltpu.VMEM(table.shape, BF16),
            wide_scratch(modes_shape, channels),
            pltpu.SemaphoreType.DMA((block_rows // rows + 1,)),
        ],
        compiler_params=params(24),
    )(in_hbm(fields), in_hbm(table))


def local_kernel(field_ref, weight_ref, out_ref):
    out_ref[...] = dot(weight_ref[...], field_ref[...], ((1,), (0,))).astype(BF16)


def local_mix(field, weight):
    block = pl.BlockSpec((weight.shape[0], field.shape[1]), lambda g: (g, 0))
    return pl.pallas_call(
        local_kernel,
        grid=(field.shape[0] // weight.shape[0],),
        in_specs=[block, pl.BlockSpec(weight.shape, lambda g: (0, 0))],
        out_specs=block,
        out_shape=pltpu.HBM(field.shape, BF16),
        compiler_params=params(16),
    )(in_hbm(field), weight)


def middle_kernel(
    channels, layer, values_ref, weights_ref, forward_ref, backward_ref, out_ref, weight_ref, sem
):
    kept = forward_ref.shape[0] // 2
    lanes = 2 * channels
    per_device = weight_ref.shape[0]
    own = pl.ds(lax.axis_index("lat") * per_device, per_device)
    read = pltpu.make_async_copy(weights_ref.at[layer, own], weight_ref, sem)
    read.start()
    products = dot(forward_ref[...], values_ref[...], ((1,), (0,)))
    low = low_half((kept, lanes), channels)
    low_w = low_half((channels, lanes), channels)
    read.wait()
    for k in range(per_device):
        part = slice(k * lanes, (k + 1) * lanes)
        turned = pltpu.roll(products[kept:, part], channels, 1)
        modes = (products[:kept, part] + jnp.where(low, turned, -turned)).astype(BF16)
        weight = weight_ref[k].astype(F32)
        swapped = pltpu.roll(weight, channels, 1)
        mixing = jnp.concatenate([weight, jnp.where(low_w, -swapped, swapped)], axis=0)
        mixed = dot(modes, mixing.astype(BF16), ((1,), (0,)))
        swapped = pltpu.roll(mixed, channels, 1)
        both = jnp.concatenate([mixed, jnp.where(low, -swapped, swapped)], axis=0).astype(BF16)
        out_ref[:, part] = dot(backward_ref[...], both, ((1,), (0,))).astype(BF16)


def middle(values, weights, layer, forward, backward, channels):
    per_device = values.shape[1] // (2 * channels)
    return pl.pallas_call(
        functools.partial(middle_kernel, channels, layer),
        in_specs=[RESIDENT, OUTSIDE, RESIDENT, RESIDENT],
        out_specs=RESIDENT,
        out_shape=pltpu.VMEM(values.shape, BF16),
        scratch_shapes=[
            pltpu.VMEM((per_device,) + weights.shape[2:], BF16),
            pltpu.SemaphoreType.DMA(()),
        ],
        compiler_params=params(24),
    )(in_vmem(values), in_hbm(weights), in_vmem(forward), in_vmem(backward))


def gelu_of_double(v):
    scale = math.sqrt(2.0 / math.pi)
    return v * jnp.tanh(v * (BF16(2.0 * scale) + BF16(8.0 * 0.044715 * scale) * (v * v))) + v


def spectral_block(modes, back_ref, local_ref, out_ref, first):
    lon_count = back_ref.shape[1]
    chunk = min(256, lon_count)
    rows = slice(first, first + modes.shape[0])
    for start in range(0, lon_count, chunk):
        part = slice(start, start + chunk)
        total = dot(modes, back_ref[:, part], ((1,), (0,))) + local_ref[rows, part].astype(F32)
        local_ref[rows, part] = total.astype(BF16)
    out_ref[rows, :] = gelu_of_double(local_ref[rows, :])


def row_copies(source_ref, target_ref, sems, steps):
    block = source_ref.shape[0] // steps
    parts = [pl.ds(step * block, block) for step in range(steps)]
    return [
        pltpu.make_async_copy(source_ref.at[part], target_ref.at[part], sems.at[step])
        for step, part in enumerate(parts)
    ]


def back_kernel(
    block_rows, channels, devices, rows, kind, modes_ref, local_ref, back_ref, *rest
):
    if kind == "field":
        out_ref, *rest = rest
    else:
        extra_ref, out_ref, *rest = rest
    local_copy, field_ref, wide_ref, lhs_ref, in_sems, out_sems, *rest = rest
    steps, block = block_rows // rows, rows * channels
    arriving = row_copies(local_ref, local_copy, in_sems, steps)
    leaving = []
    if kind != "modes":
        leaving = row_copies(field_ref, out_ref, out_sems, steps)
    for copy in arriving:
        copy.start()
    unpack(modes_ref, wide_ref)
    for step in range(steps):
        modes = gather_modes(wide_ref, step * rows, rows, block_rows, channels, devices)
        lhs_ref[step * block : (step + 1) * block, :] = modes.T.astype(BF16)
    for step in range(steps):
        part = slice(step * block, (step + 1) * block)
        arriving[step].wait()
        spectral_block(lhs_ref[part, :], back_ref, local_copy, field_ref, step * block)
        if kind == "modes":
            product = dot(extra_ref[...], field_ref[part, :], ((1,), (1,)))
            scatter_modes(product, rest[0], step * rows, rows, block_rows, channels, devices)
        if kind == "mix":
            unit = extra_ref.shape[0]
            for start in range(step * block, (step + 1) * block, unit):
                piece = slice(start, start + unit)
                mixed = dot(extra_ref[...], field_ref[piece, :], ((1,), (0,)))
                field_ref[piece, :] = mixed.astype(BF16)
        if leaving:
            leaving[step].start()
    if kind == "modes":
        pack(rest[0], out_ref)
    for copy in leaving:
        copy.wait()


def back_transform(kind, modes, local, back, extra, block_rows, channels, devices, rows):
    steps = block_rows // rows
    scratch = [
        pltpu.VMEM(local.shape, BF16),
        pltpu.VMEM(local.shape, BF16),
        wide_scratch(modes.shape, channels),
        pltpu.VMEM((local.shape[0], back.shape[0]), BF16),
        pltpu.SemaphoreType.DMA((steps,)),
        pltpu.SemaphoreType.DMA((steps,)),
    ]
    args = [in_vmem(modes), in_hbm(local), in_vmem(back)]
    if kind != "field":
        args.append(in_vmem(extra))
    if kind == "modes":
        scratch.append(wide_scratch(modes.shape, channels))
    return pl.pallas_call(
        functools.partial(back_kernel, block_rows, channels, devices, rows, kind),
        in_specs=[RESIDENT, OUTSIDE] + [RESIDENT] * (len(args) - 2),
        out_specs=RESIDENT if kind == "modes" else OUTSIDE,
        out_shape=pltpu.VMEM(modes.shape, BF16)
        if kind == "modes"
        else pltpu.HBM(local.shape, BF16),
        scratch_shapes=scratch,
        compiler_params=params(32),
    )(*args)


def exchange(array, devices):
    parts = array.reshape(devices, array.shape[0] // devices, array.shape[1])
    return lax.all_to_all(parts, "lat", 0, 0, tiled=True).reshape(array.shape)


def shards(fields, spectral_weight, local_weight):
    block_rows, channels, lon_count = fields.shape
    layer_count, mode_count = spectral_weight.shape[:2]
    devices = lax.axis_size("lat")
    rows = max(2, 256 // channels)
    forward_lon, backward_lon = lon_tables(lon_count, mode_count, devices)
    forward_lat, backward_lat = lat_tables(block_rows * devices, KY, block_rows)
    mixers = jnp.einsum(
        "rs,lcd->lrdsc", 0.5 * jnp.eye(rows, dtype=BF16), local_weight
    ).reshape(layer_count, rows * channels, rows * channels)
    wide_rows = 2 * rows if block_rows % (2 * rows) == 0 else rows
    sizes = dict(block_rows=block_rows, channels=channels, devices=devices, rows=wide_rows)
    field = fields.reshape(block_rows * channels, lon_count)
    modes = first_transform(field, forward_lon, **sizes)
    local = local_mix(field, mixers[0])
    for layer in range(layer_count):
        arrived = exchange(modes, devices)
        rebuilt = middle(arrived, spectral_weight, layer, forward_lat, backward_lat, channels)
        returned = exchange(rebuilt, devices)
        end = functools.partial(back_transform, modes=returned, local=local, back=backward_lon)
        if layer < layer_count - 1:
            modes = end("modes", extra=forward_lon, **sizes)
            local = end("mix", extra=mixers[layer + 1], **sizes)
        else:
            field = end("field", extra=None, **sizes)
    return field.reshape(fields.shape)


def solution(mesh):
    return jax.shard_map(
        shards,
        mesh=mesh,
        in_specs=(P(("grp", "lat"), None, None), P(), P()),
        out_specs=P(("grp", "lat"), None, None),
        check_vma=False,
    )
```

```python
import functools
import math

import jax
import jax.numpy as jnp
import ml_dtypes
import numpy as np
from jax import lax
from jax.experimental import pallas as pl
from jax.experimental.pallas import tpu as pltpu
from jax.sharding import PartitionSpec as P

KY = 128
F32 = jnp.float32
BF16 = jnp.bfloat16


def rounded(table):
    return np.asarray(table, np.float32).astype(ml_dtypes.bfloat16)


def mode_order(mode_count, devices):
    per_device = mode_count // devices
    return np.arange(mode_count).reshape(devices, per_device).T.reshape(-1)


def lon_tables(lon_count, mode_count, devices):
    modes = mode_order(mode_count, devices).astype(np.int64)[:, None]
    cells = np.arange(lon_count, dtype=np.int64)[None, :]
    angle = 2.0 * np.pi / lon_count * (cells * modes % lon_count)
    both = np.concatenate([np.cos(angle), -np.sin(angle)], axis=0)
    return (rounded(both / math.sqrt(lon_count)), rounded(both / math.sqrt(mode_count) * 0.5))


def lat_tables(lat_count, kept_count, block_rows):
    index = np.arange(kept_count, dtype=np.int64)
    waves = np.where(index < kept_count // 2, index, lat_count - kept_count + index)
    rowids = np.arange(lat_count, dtype=np.int64)
    latitudes = rowids % block_rows * (lat_count // block_rows) + rowids // block_rows
    angle = 2.0 * np.pi / lat_count * (waves[:, None] * latitudes[None, :] % lat_count)
    both = np.concatenate([np.cos(angle), np.sin(angle)], axis=0)
    return (rounded(both / math.sqrt(lat_count)), rounded(both.T / math.sqrt(kept_count)))


def low_half(shape, channels):
    return lax.broadcasted_iota(jnp.int32, shape, len(shape) - 1) % (2 * channels) < channels


def dot(a, b, dims):
    return lax.dot_general(a, b, (dims, ((), ())), preferred_element_type=F32)


def scatter_modes(modes_out, wide_ref, first_row, rows, block_rows, channels, devices):
    half = modes_out.shape[0] // 2
    per_device = half // devices
    lanes = 2 * channels
    low = low_half((half, lanes), channels)
    for pair in range(rows // 2):
        real = modes_out[:half, pair * lanes : (pair + 1) * lanes]
        imag = modes_out[half:, pair * lanes : (pair + 1) * lanes]
        even = jnp.where(low, real, pltpu.roll(imag, channels, 1))
        odd = jnp.where(low, pltpu.roll(real, channels, 1), imag)
        for offset, values in ((0, even), (1, odd)):
            row = first_row + 2 * pair + offset
            for k in range(per_device):
                wide_ref[k, pl.ds(row, devices, stride=block_rows), :] = values[
                    k * devices : (k + 1) * devices
                ]


def gather_modes(wide_ref, first_row, rows, block_rows, channels, devices):
    lanes = 2 * channels
    per_device = wide_ref.shape[0]
    low = low_half((per_device * devices, lanes), channels)
    reals, imags = [], []
    for pair in range(rows // 2):
        even, odd = [
            jnp.concatenate(
                [
                    wide_ref[
                        k, pl.ds(first_row + 2 * pair + offset, devices, stride=block_rows), :
                    ]
                    for k in range(per_device)
                ],
                axis=0,
            )
            for offset in range(2)
        ]
        reals.append(jnp.where(low, even, pltpu.roll(odd, channels, 1)))
        imags.append(jnp.where(low, pltpu.roll(even, channels, 1), odd))
    return jnp.concatenate(
        [jnp.concatenate(reals, axis=1), jnp.concatenate(imags, axis=1)], axis=0
    )


def pack(wide_ref, out_ref):
    lanes = wide_ref.shape[2]
    for k in range(wide_ref.shape[0]):
        out_ref[:, k * lanes : (k + 1) * lanes] = wide_ref[k].astype(BF16)


def unpack(in_ref, wide_ref):
    lanes = wide_ref.shape[2]
    for k in range(wide_ref.shape[0]):
        wide_ref[k] = in_ref[:, k * lanes : (k + 1) * lanes].astype(F32)


def wide_scratch(shape, channels):
    return pltpu.VMEM((shape[1] // (2 * channels), shape[0], 2 * channels), F32)


def in_vmem(array):
    return pltpu.with_memory_space_constraint(array, pltpu.VMEM)


def in_hbm(array):
    return pltpu.with_memory_space_constraint(array, pltpu.HBM)


def params(limit):
    return pltpu.CompilerParams(vmem_limit_bytes=limit * 2**20)


OUTSIDE = pl.BlockSpec(memory_space=pltpu.HBM)
RESIDENT = pl.BlockSpec(memory_space=pltpu.VMEM)


def first_kernel(
    block_rows, channels, devices, rows,
    fields_ref, table_ref, weights_ref, modes_ref, own_ref, copy_ref, table_copy, wide_ref, sems,
):
    steps, block = block_rows // rows, rows * channels
    table_read = pltpu.make_async_copy(table_ref, table_copy, sems.at[steps])
    per_device = own_ref.shape[1]
    own = pl.ds(lax.axis_index("lat") * per_device, per_device)
    own_read = pltpu.make_async_copy(weights_ref.at[:, own], own_ref, sems.at[steps + 1])

    def read(step):
        part = pl.ds(step * block, block)
        return pltpu.make_async_copy(fields_ref.at[part], copy_ref.at[part], sems.at[step])

    table_read.start()
    for step in range(steps):
        read(step).start()
    own_read.start()
    table_read.wait()

    def body(step, carry):
        read(step).wait()
        field = copy_ref[pl.ds(pl.multiple_of(step * block, block), block), :]
        modes = dot(table_copy[...], field, ((1,), (1,)))
        scatter_modes(modes, wide_ref, step * rows, rows, block_rows, channels, devices)
        return carry

    lax.fori_loop(0, steps, body, 0)
    own_read.wait()
    pack(wide_ref, modes_ref)


def first_transform(fields, table, weights, block_rows, channels, devices, rows):
    per_device = weights.shape[1] // devices
    own_shape = (weights.shape[0], per_device) + weights.shape[2:]
    modes_shape = (devices * block_rows, table.shape[0] // devices * channels)
    return pl.pallas_call(
        functools.partial(first_kernel, block_rows, channels, devices, rows),
        in_specs=[OUTSIDE, OUTSIDE, OUTSIDE],
        out_specs=[RESIDENT, RESIDENT],
        out_shape=[pltpu.VMEM(modes_shape, BF16), pltpu.VMEM(own_shape, BF16)],
        scratch_shapes=[
            pltpu.VMEM(fields.shape, BF16),
            pltpu.VMEM(table.shape, BF16),
            wide_scratch(modes_shape, channels),
            pltpu.SemaphoreType.DMA((block_rows // rows + 2,)),
        ],
        compiler_params=params(24),
    )(in_hbm(fields), in_hbm(table), in_hbm(weights))


def local_kernel(field_ref, weight_ref, out_ref):
    out_ref[...] = dot(weight_ref[...], field_ref[...], ((1,), (0,))).astype(BF16)


def local_mix(field, weight):
    block = pl.BlockSpec((weight.shape[0], field.shape[1]), lambda g: (g, 0))
    return pl.pallas_call(
        local_kernel,
        grid=(field.shape[0] // weight.shape[0],),
        in_specs=[block, pl.BlockSpec(weight.shape, lambda g: (0, 0))],
        out_specs=block,
        out_shape=pltpu.HBM(field.shape, BF16),
        compiler_params=params(16),
    )(in_hbm(field), weight)


def middle_kernel(
    channels, layer, values_ref, weights_ref, forward_ref, backward_ref, out_ref, copy_ref, sems
):
    kept = forward_ref.shape[0] // 2
    lanes = 2 * channels
    per_device = weights_ref.shape[1]
    products = dot(forward_ref[...], values_ref[...], ((1,), (0,)))
    low = low_half((kept, lanes), channels)
    low_w = low_half((channels, lanes), channels)
    writes = []
    for k in range(per_device):
        part = slice(k * lanes, (k + 1) * lanes)
        turned = pltpu.roll(products[kept:, part], channels, 1)
        modes = (products[:kept, part] + jnp.where(low, turned, -turned)).astype(BF16)
        weight = weights_ref[layer, k].astype(F32)
        swapped = pltpu.roll(weight, channels, 1)
        mixing = jnp.concatenate([weight, jnp.where(low_w, -swapped, swapped)], axis=0)
        mixed = dot(modes, mixing.astype(BF16), ((1,), (0,)))
        swapped = pltpu.roll(mixed, channels, 1)
        both = jnp.concatenate([mixed, jnp.where(low, -swapped, swapped)], axis=0).astype(BF16)
        copy_ref[k] = dot(backward_ref[...], both, ((1,), (0,))).astype(BF16)
        target = out_ref.at[:, pl.ds(k * lanes, lanes)]
        writes.append(pltpu.make_async_copy(copy_ref.at[k], target, sems.at[k]))
        writes[-1].start()
    for write in writes:
        write.wait()


def middle(values, weights, layer, forward, backward, channels):
    per_device = weights.shape[1]
    return pl.pallas_call(
        functools.partial(middle_kernel, channels, layer),
        in_specs=[RESIDENT] * 4,
        out_specs=OUTSIDE,
        out_shape=pltpu.HBM(values.shape, BF16),
        scratch_shapes=[
            pltpu.VMEM((per_device, values.shape[0], 2 * channels), BF16),
            pltpu.SemaphoreType.DMA((per_device,)),
        ],
        compiler_params=params(24),
    )(in_vmem(values), in_vmem(weights), in_vmem(forward), in_vmem(backward))


def gelu_of_double(v):
    scale = math.sqrt(2.0 / math.pi)
    return v * jnp.tanh(v * (BF16(2.0 * scale) + BF16(8.0 * 0.044715 * scale) * (v * v))) + v


def back_kernel(
    block_rows, channels, devices, rows, kind, modes_ref, local_ref, back_ref, *rest
):
    if kind == "field":
        out_ref, *rest = rest
    else:
        extra_ref, out_ref, *rest = rest
    local_copy, field_ref, wide_ref, lhs_ref, in_sems, out_sems, *rest = rest
    steps, block = block_rows // rows, rows * channels
    lon_count = back_ref.shape[1]
    chunk = min(256, lon_count)

    def arriving(step):
        part = pl.ds(step * block, block)
        return pltpu.make_async_copy(local_ref.at[part], local_copy.at[part], in_sems.at[step])

    def leaving(step):
        part = pl.ds(step * block, block)
        return pltpu.make_async_copy(field_ref.at[part], out_ref.at[part], out_sems.at[step])

    for step in range(steps):
        arriving(step).start()
    unpack(modes_ref, wide_ref)
    few = math.gcd(rows, max(2, 256 // channels))

    def relayout(step, carry):
        modes = gather_modes(wide_ref, step * few, few, block_rows, channels, devices)
        size = few * channels
        lhs_ref[pl.ds(pl.multiple_of(step * size, size), size), :] = modes.T.astype(BF16)
        return carry

    lax.fori_loop(0, block_rows // few, relayout, 0)

    def body(step, carry):
        first = step * block if isinstance(step, int) else pl.multiple_of(step * block, block)
        part = pl.ds(first, block)
        arriving(step).wait()
        for start in range(0, lon_count, chunk):
            lons = slice(start, start + chunk)
            total = dot(lhs_ref[part, :], back_ref[:, lons], ((1,), (0,))).astype(BF16)
            field_ref[part, lons] = gelu_of_double(total + local_copy[part, lons])
        if kind == "modes":
            product = dot(extra_ref[...], field_ref[part, :], ((1,), (1,)))
            scatter_modes(product, rest[0], step * rows, rows, block_rows, channels, devices)
        if kind == "mix":
            unit = extra_ref.shape[0]
            for start in range(0, block, unit):
                piece = pl.ds(first + start, unit)
                mixed = dot(extra_ref[...], field_ref[piece, :], ((1,), (0,)))
                field_ref[piece, :] = mixed.astype(BF16)
        if kind != "modes":
            leaving(step).start()
        return carry

    if kind == "field":
        lax.fori_loop(0, steps, body, 0)
    else:
        for step in range(steps):
            body(step, 0)
    if kind == "modes":
        pack(rest[0], out_ref)
    else:
        for step in range(steps):
            leaving(step).wait()


def back_transform(kind, modes, local, back, extra, block_rows, channels, devices, rows):
    steps = block_rows // rows
    scratch = [
        pltpu.VMEM(local.shape, BF16),
        pltpu.VMEM(local.shape, BF16),
        wide_scratch(modes.shape, channels),
        pltpu.VMEM((local.shape[0], back.shape[0]), BF16),
        pltpu.SemaphoreType.DMA((steps,)),
        pltpu.SemaphoreType.DMA((steps,)),
    ]
    args = [in_vmem(modes), in_hbm(local), in_vmem(back)]
    if kind != "field":
        args.append(in_vmem(extra))
    if kind == "modes":
        scratch.append(wide_scratch(modes.shape, channels))
    return pl.pallas_call(
        functools.partial(back_kernel, block_rows, channels, devices, rows, kind),
        in_specs=[RESIDENT, OUTSIDE] + [RESIDENT] * (len(args) - 2),
        out_specs=RESIDENT if kind == "modes" else OUTSIDE,
        out_shape=pltpu.VMEM(modes.shape, BF16)
        if kind == "modes"
        else pltpu.HBM(local.shape, BF16),
        scratch_shapes=scratch,
        compiler_params=params(32),
    )(*args)


def exchange(array, devices):
    parts = array.reshape(devices, array.shape[0] // devices, array.shape[1])
    return lax.all_to_all(parts, "lat", 0, 0, tiled=True).reshape(array.shape)


def shards(fields, spectral_weight, local_weight):
    block_rows, channels, lon_count = fields.shape
    layer_count, mode_count = spectral_weight.shape[:2]
    devices = lax.axis_size("lat")
    rows = max(2, 256 // channels)
    forward_lon, backward_lon = lon_tables(lon_count, mode_count, devices)
    forward_lat, backward_lat = lat_tables(block_rows * devices, KY, block_rows)
    mixers = jnp.einsum(
        "rs,lcd->lrdsc", 0.5 * jnp.eye(rows, dtype=BF16), local_weight
    ).reshape(layer_count, rows * channels, rows * channels)
    wide_rows = 2 * rows if block_rows % (2 * rows) == 0 else rows
    sizes = dict(block_rows=block_rows, channels=channels, devices=devices, rows=wide_rows)
    field = fields.reshape(block_rows * channels, lon_count)
    modes, weights = first_transform(field, forward_lon, spectral_weight, **sizes)
    local = local_mix(field, mixers[0])
    for layer in range(layer_count):
        arrived = exchange(modes, devices)
        rebuilt = middle(arrived, weights, layer, forward_lat, backward_lat, channels)
        returned = exchange(rebuilt, devices)
        end = functools.partial(back_transform, modes=returned, local=local, back=backward_lon)
        if layer < layer_count - 1:
            modes = end("modes", extra=forward_lon, **sizes)
            local = end("mix", extra=mixers[layer + 1], **sizes)
        else:
            field = end("field", extra=None, **{**sizes, "rows": rows})
    return field.reshape(fields.shape)


def solution(mesh):
    return jax.shard_map(
        shards,
        mesh=mesh,
        in_specs=(P(("grp", "lat"), None, None), P(), P()),
        out_specs=P(("grp", "lat"), None, None),
        check_vma=False,
    )
```

```python
import functools
import math

import jax
import jax.numpy as jnp
import ml_dtypes
import numpy as np
from jax import lax
from jax.experimental import pallas as pl
from jax.experimental.pallas import tpu as pltpu
from jax.sharding import PartitionSpec as P

KY = 128
F32 = jnp.float32
BF16 = jnp.bfloat16


def rounded(table):
    return np.asarray(table, np.float32).astype(ml_dtypes.bfloat16)


def mode_order(mode_count, devices):
    per_device = mode_count // devices
    return np.arange(mode_count).reshape(devices, per_device).T.reshape(-1)


def lon_tables(lon_count, mode_count, devices):
    modes = mode_order(mode_count, devices).astype(np.int64)[:, None]
    cells = np.arange(lon_count, dtype=np.int64)[None, :]
    angle = 2.0 * np.pi / lon_count * (cells * modes % lon_count)
    both = np.concatenate([np.cos(angle), -np.sin(angle)], axis=0)
    return (rounded(both / math.sqrt(lon_count)), rounded(both / math.sqrt(mode_count) * 0.5))


def lat_tables(lat_count, kept_count, block_rows):
    index = np.arange(kept_count, dtype=np.int64)
    waves = np.where(index < kept_count // 2, index, lat_count - kept_count + index)
    rowids = np.arange(lat_count, dtype=np.int64)
    latitudes = rowids % block_rows * (lat_count // block_rows) + rowids // block_rows
    angle = 2.0 * np.pi / lat_count * (waves[:, None] * latitudes[None, :] % lat_count)
    both = np.concatenate([np.cos(angle), np.sin(angle)], axis=0)
    return (rounded(both / math.sqrt(lat_count)), rounded(both.T / math.sqrt(kept_count)))


def low_half(shape, channels):
    return lax.broadcasted_iota(jnp.int32, shape, len(shape) - 1) % (2 * channels) < channels


def dot(a, b, dims):
    return lax.dot_general(a, b, (dims, ((), ())), preferred_element_type=F32)


def scatter_modes(modes_out, wide_ref, first_row, rows, block_rows, channels, devices):
    half = modes_out.shape[0] // 2
    per_device = half // devices
    lanes = 2 * channels
    low = low_half((half, lanes), channels)
    for pair in range(rows // 2):
        real = modes_out[:half, pair * lanes : (pair + 1) * lanes]
        imag = modes_out[half:, pair * lanes : (pair + 1) * lanes]
        even = jnp.where(low, real, pltpu.roll(imag, channels, 1))
        odd = jnp.where(low, pltpu.roll(real, channels, 1), imag)
        for offset, values in ((0, even), (1, odd)):
            row = first_row + 2 * pair + offset
            for k in range(per_device):
                wide_ref[k, pl.ds(row, devices, stride=block_rows), :] = values[
                    k * devices : (k + 1) * devices
                ]


def gather_modes(wide_ref, first_row, rows, block_rows, channels, devices):
    lanes = 2 * channels
    per_device = wide_ref.shape[0]
    low = low_half((per_device * devices, lanes), channels)
    reals, imags = [], []
    for pair in range(rows // 2):
        even, odd = [
            jnp.concatenate(
                [
                    wide_ref[
                        k, pl.ds(first_row + 2 * pair + offset, devices, stride=block_rows), :
                    ]
                    for k in range(per_device)
                ],
                axis=0,
            )
            for offset in range(2)
        ]
        reals.append(jnp.where(low, even, pltpu.roll(odd, channels, 1)))
        imags.append(jnp.where(low, pltpu.roll(even, channels, 1), odd))
    return jnp.concatenate(
        [jnp.concatenate(reals, axis=1), jnp.concatenate(imags, axis=1)], axis=0
    )


def pack(wide_ref, out_ref):
    lanes = wide_ref.shape[2]
    for k in range(wide_ref.shape[0]):
        out_ref[:, k * lanes : (k + 1) * lanes] = wide_ref[k].astype(BF16)


def unpack(in_ref, wide_ref):
    lanes = wide_ref.shape[2]
    for k in range(wide_ref.shape[0]):
        wide_ref[k] = in_ref[:, k * lanes : (k + 1) * lanes].astype(F32)


def wide_scratch(shape, channels):
    return pltpu.VMEM((shape[1] // (2 * channels), shape[0], 2 * channels), F32)


def in_vmem(array):
    return pltpu.with_memory_space_constraint(array, pltpu.VMEM)


def in_hbm(array):
    return pltpu.with_memory_space_constraint(array, pltpu.HBM)


def params(limit):
    return pltpu.CompilerParams(vmem_limit_bytes=limit * 2**20)


OUTSIDE = pl.BlockSpec(memory_space=pltpu.HBM)
RESIDENT = pl.BlockSpec(memory_space=pltpu.VMEM)


def first_kernel(
    block_rows, channels, devices, rows,
    fields_ref, table_ref, weights_ref, modes_ref, own_ref, copy_ref, table_copy, wide_ref, sems,
):
    steps, block = block_rows // rows, rows * channels
    table_read = pltpu.make_async_copy(table_ref, table_copy, sems.at[steps])
    per_device = own_ref.shape[1]
    own = pl.ds(lax.rem(lax.axis_index("lat"), devices) * per_device, per_device)
    own_read = pltpu.make_async_copy(weights_ref.at[:, own], own_ref, sems.at[steps + 1])

    def read(step):
        part = pl.ds(step * block, block)
        return pltpu.make_async_copy(fields_ref.at[part], copy_ref.at[part], sems.at[step])

    table_read.start()
    for step in range(steps):
        read(step).start()
    own_read.start()
    table_read.wait()

    def body(step, carry):
        read(step).wait()
        field = copy_ref[pl.ds(pl.multiple_of(step * block, block), block), :]
        modes = dot(table_copy[...], field, ((1,), (1,)))
        scatter_modes(modes, wide_ref, step * rows, rows, block_rows, channels, devices)
        return carry

    lax.fori_loop(0, steps, body, 0)
    own_read.wait()
    pack(wide_ref, modes_ref)


def first_transform(fields, table, weights, block_rows, channels, devices, rows):
    per_device = weights.shape[1] // devices
    own_shape = (weights.shape[0], per_device) + weights.shape[2:]
    modes_shape = (devices * block_rows, table.shape[0] // devices * channels)
    return pl.pallas_call(
        functools.partial(first_kernel, block_rows, channels, devices, rows),
        in_specs=[OUTSIDE, OUTSIDE, OUTSIDE],
        out_specs=[RESIDENT, RESIDENT],
        out_shape=[pltpu.VMEM(modes_shape, BF16), pltpu.VMEM(own_shape, BF16)],
        scratch_shapes=[
            pltpu.VMEM(fields.shape, BF16),
            pltpu.VMEM(table.shape, BF16),
            wide_scratch(modes_shape, channels),
            pltpu.SemaphoreType.DMA((block_rows // rows + 2,)),
        ],
        compiler_params=params(24),
    )(in_hbm(fields), in_hbm(table), in_hbm(weights))


def local_kernel(field_ref, weight_ref, out_ref):
    out_ref[...] = dot(weight_ref[...], field_ref[...], ((1,), (0,))).astype(BF16)


def local_mix(field, weight):
    block = pl.BlockSpec((weight.shape[0], field.shape[1]), lambda g: (g, 0))
    return pl.pallas_call(
        local_kernel,
        grid=(field.shape[0] // weight.shape[0],),
        in_specs=[block, pl.BlockSpec(weight.shape, lambda g: (0, 0))],
        out_specs=block,
        out_shape=pltpu.HBM(field.shape, BF16),
        compiler_params=params(16),
    )(in_hbm(field), weight)


def partial_kernel(channels, first, values_ref, forward_ref, out_ref):
    kept = forward_ref.shape[1] // 2
    lanes = 2 * channels
    half = lax.axis_index("lat") * forward_ref.shape[0] // lax.axis_size("lat")
    columns = slice(first * lanes, first * lanes + out_ref.shape[1])
    products = dot(forward_ref[half], values_ref[:, columns], ((1,), (0,)))
    low = low_half((kept, lanes), channels)
    for start in range(0, out_ref.shape[1], lanes):
        part = slice(start, start + lanes)
        turned = pltpu.roll(products[kept:, part], channels, 1)
        sums = products[:kept, part] + jnp.where(low, turned, -turned)
        out_ref[:, part] = sums.astype(BF16)


def partial_sums(values, forward, first, count, channels):
    shape = (forward.shape[1] // 2, count * 2 * channels)
    return pl.pallas_call(
        functools.partial(partial_kernel, channels, first),
        in_specs=[RESIDENT] * 2,
        out_specs=RESIDENT,
        out_shape=jax.ShapeDtypeStruct(shape, BF16),
        compiler_params=params(24),
    )(in_vmem(values), in_vmem(forward))


def middle_kernel(
    channels, layer, first, own_ref, other_ref, weights_ref, backward_ref, *rest
):
    out_ref, copy_ref, sems = rest[-3:]
    kept = own_ref.shape[0]
    lanes = 2 * channels
    half = lax.axis_index("lat") * backward_ref.shape[0] // lax.axis_size("lat")
    low = low_half((kept, lanes), channels)
    low_w = low_half((channels, lanes), channels)
    writes = []
    for k in range(own_ref.shape[1] // lanes):
        part = slice(k * lanes, (k + 1) * lanes)
        modes = (own_ref[:, part].astype(F32) + other_ref[:, part].astype(F32)).astype(BF16)
        weight = weights_ref[layer, first + k].astype(F32)
        swapped = pltpu.roll(weight, channels, 1)
        mixing = jnp.concatenate([weight, jnp.where(low_w, -swapped, swapped)], axis=0)
        mixed = dot(modes, mixing.astype(BF16), ((1,), (0,)))
        swapped = pltpu.roll(mixed, channels, 1)
        both = jnp.concatenate([mixed, jnp.where(low, -swapped, swapped)], axis=0).astype(BF16)
        copy_ref[k] = dot(backward_ref[half], both, ((1,), (0,))).astype(BF16)
        target = out_ref.at[:, pl.ds((first + k) * lanes, lanes)]
        writes.append(pltpu.make_async_copy(copy_ref.at[k], target, sems.at[k]))
        writes[-1].start()
    for write in writes:
        write.wait()


def middle(own, other, weights, layer, first, backward, so_far, channels):
    count = own.shape[1] // (2 * channels)
    rows = backward.shape[1]
    args = [in_vmem(own), in_vmem(other), in_vmem(weights), in_vmem(backward)]
    specs = [RESIDENT] * 4
    if so_far is not None:
        args.append(in_hbm(so_far))
        specs.append(OUTSIDE)
    return pl.pallas_call(
        functools.partial(middle_kernel, channels, layer, first),
        in_specs=specs,
        out_specs=OUTSIDE,
        out_shape=pltpu.HBM((rows, weights.shape[1] * 2 * channels), BF16),
        scratch_shapes=[
            pltpu.VMEM((count, rows, 2 * channels), BF16),
            pltpu.SemaphoreType.DMA((count,)),
        ],
        input_output_aliases={} if so_far is None else {4: 0},
        compiler_params=params(24),
    )(*args)


def gelu_of_double(v):
    scale = math.sqrt(2.0 / math.pi)
    return v * jnp.tanh(v * (BF16(2.0 * scale) + BF16(8.0 * 0.044715 * scale) * (v * v))) + v


def back_kernel(
    block_rows, channels, devices, rows, kind, modes_ref, local_ref, back_ref, *rest
):
    if kind == "field":
        out_ref, *rest = rest
    else:
        extra_ref, out_ref, *rest = rest
    local_copy, field_ref, wide_ref, lhs_ref, in_sems, out_sems, *rest = rest
    steps, block = block_rows // rows, rows * channels
    lon_count = back_ref.shape[1]
    chunk = min(256, lon_count)

    def arriving(step):
        part = pl.ds(step * block, block)
        return pltpu.make_async_copy(local_ref.at[part], local_copy.at[part], in_sems.at[step])

    def leaving(step):
        part = pl.ds(step * block, block)
        return pltpu.make_async_copy(field_ref.at[part], out_ref.at[part], out_sems.at[step])

    for step in range(steps):
        arriving(step).start()
    unpack(modes_ref, wide_ref)
    few = math.gcd(rows, max(2, 256 // channels))

    def relayout(step, carry):
        modes = gather_modes(wide_ref, step * few, few, block_rows, channels, devices)
        size = few * channels
        lhs_ref[pl.ds(pl.multiple_of(step * size, size), size), :] = modes.T.astype(BF16)
        return carry

    lax.fori_loop(0, block_rows // few, relayout, 0)

    def body(step, carry):
        first = step * block if isinstance(step, int) else pl.multiple_of(step * block, block)
        part = pl.ds(first, block)
        arriving(step).wait()
        for start in range(0, lon_count, chunk):
            lons = slice(start, start + chunk)
            total = dot(lhs_ref[part, :], back_ref[:, lons], ((1,), (0,))).astype(BF16)
            field_ref[part, lons] = gelu_of_double(total + local_copy[part, lons])
        if kind == "modes":
            product = dot(extra_ref[...], field_ref[part, :], ((1,), (1,)))
            scatter_modes(product, rest[0], step * rows, rows, block_rows, channels, devices)
        if kind == "mix":
            unit = extra_ref.shape[0]
            for start in range(0, block, unit):
                piece = pl.ds(first + start, unit)
                mixed = dot(extra_ref[...], field_ref[piece, :], ((1,), (0,)))
                field_ref[piece, :] = mixed.astype(BF16)
        if kind != "modes":
            leaving(step).start()
        return carry

    if kind == "field":
        lax.fori_loop(0, steps, body, 0)
    else:
        for step in range(steps):
            body(step, 0)
    if kind == "modes":
        pack(rest[0], out_ref)
    else:
        for step in range(steps):
            leaving(step).wait()


def back_transform(kind, modes, local, back, extra, block_rows, channels, devices, rows):
    steps = block_rows // rows
    scratch = [
        pltpu.VMEM(local.shape, BF16),
        pltpu.VMEM(local.shape, BF16),
        wide_scratch(modes.shape, channels),
        pltpu.VMEM((local.shape[0], back.shape[0]), BF16),
        pltpu.SemaphoreType.DMA((steps,)),
        pltpu.SemaphoreType.DMA((steps,)),
    ]
    args = [in_vmem(modes), in_hbm(local), in_vmem(back)]
    if kind != "field":
        args.append(in_vmem(extra))
    if kind == "modes":
        scratch.append(wide_scratch(modes.shape, channels))
    return pl.pallas_call(
        functools.partial(back_kernel, block_rows, channels, devices, rows, kind),
        in_specs=[RESIDENT, OUTSIDE] + [RESIDENT] * (len(args) - 2),
        out_specs=RESIDENT if kind == "modes" else OUTSIDE,
        out_shape=pltpu.VMEM(modes.shape, BF16)
        if kind == "modes"
        else pltpu.HBM(local.shape, BF16),
        scratch_shapes=scratch,
        compiler_params=params(32),
    )(*args)


def exchange(array, peers, devices):
    parts = array.reshape(peers, array.shape[0] // peers, array.shape[1])
    groups = [list(range(start, start + peers)) for start in range(0, devices, peers)]
    moved = lax.all_to_all(parts, "lat", 0, 0, tiled=True, axis_index_groups=groups)
    return moved.reshape(array.shape)


def shards(fields, spectral_weight, local_weight):
    block_rows, channels, lon_count = fields.shape
    layer_count, mode_count = spectral_weight.shape[:2]
    devices = lax.axis_size("lat")
    rows = max(2, 256 // channels)
    peers = devices // 2
    per_device = mode_count // peers
    counts = [per_device - per_device // 2, per_device // 2]
    swap = [(source, (source + peers) % devices) for source in range(devices)]
    forward_lon, backward_lon = lon_tables(lon_count, mode_count, peers)
    forward_lat, backward_lat = lat_tables(block_rows * devices, KY, block_rows)
    forward_lat = np.stack(np.split(forward_lat, 2, axis=1))
    backward_lat = np.stack(np.split(backward_lat, 2, axis=0))
    mixers = jnp.einsum(
        "rs,lcd->lrdsc", 0.5 * jnp.eye(rows, dtype=BF16), local_weight
    ).reshape(layer_count, rows * channels, rows * channels)
    wide_rows = 2 * rows if block_rows % (2 * rows) == 0 else rows
    sizes = dict(block_rows=block_rows, channels=channels, devices=peers, rows=wide_rows)
    field = fields.reshape(block_rows * channels, lon_count)
    modes, weights = first_transform(field, forward_lon, spectral_weight, **sizes)
    local = local_mix(field, mixers[0])
    for layer in range(layer_count):
        arrived = exchange(modes, peers, devices)
        sums = []
        for first, count in zip((0, counts[0]), counts, strict=True):
            own = partial_sums(arrived, forward_lat, first, count, channels)
            sums.append((first, own, lax.ppermute(own, "lat", swap)))
        rebuilt = None
        for first, own, other in sums:
            rebuilt = middle(own, other, weights, layer, first, backward_lat, rebuilt, channels)
        returned = exchange(rebuilt, peers, devices)
        end = functools.partial(back_transform, modes=returned, local=local, back=backward_lon)
        if layer < layer_count - 1:
            modes = end("modes", extra=forward_lon, **sizes)
            local = end("mix", extra=mixers[layer + 1], **sizes)
        else:
            field = end("field", extra=None, **{**sizes, "rows": rows})
    return field.reshape(fields.shape)


def solution(mesh):
    return jax.shard_map(
        shards,
        mesh=mesh,
        in_specs=(P(("grp", "lat"), None, None), P(), P()),
        out_specs=P(("grp", "lat"), None, None),
        check_vma=False,
    )
```

```python
import functools
import math

import jax
import jax.numpy as jnp
import ml_dtypes
import numpy as np
from jax import lax
from jax.experimental import pallas as pl
from jax.experimental.pallas import tpu as pltpu
from jax.sharding import PartitionSpec as P

KY = 128
F32 = jnp.float32
BF16 = jnp.bfloat16


def rounded(table):
    return np.asarray(table, np.float32).astype(ml_dtypes.bfloat16)


def mode_order(mode_count, devices):
    per_device = mode_count // devices
    return np.arange(mode_count).reshape(devices, per_device).T.reshape(-1)


def lon_tables(lon_count, mode_count, devices):
    modes = mode_order(mode_count, devices).astype(np.int64)[:, None]
    cells = np.arange(lon_count, dtype=np.int64)[None, :]
    angle = 2.0 * np.pi / lon_count * (cells * modes % lon_count)
    both = np.concatenate([np.cos(angle), -np.sin(angle)], axis=0)
    return (rounded(both / math.sqrt(lon_count)), rounded(both / math.sqrt(mode_count) * 0.5))


def lat_tables(lat_count, kept_count, block_rows):
    index = np.arange(kept_count, dtype=np.int64)
    waves = np.where(index < kept_count // 2, index, lat_count - kept_count + index)
    rowids = np.arange(lat_count, dtype=np.int64)
    latitudes = rowids % block_rows * (lat_count // block_rows) + rowids // block_rows
    angle = 2.0 * np.pi / lat_count * (waves[:, None] * latitudes[None, :] % lat_count)
    both = np.concatenate([np.cos(angle), np.sin(angle)], axis=0)
    return (rounded(both / math.sqrt(lat_count)), rounded(both.T / math.sqrt(kept_count)))


def low_half(shape, channels):
    return lax.broadcasted_iota(jnp.int32, shape, len(shape) - 1) % (2 * channels) < channels


def dot(a, b, dims):
    return lax.dot_general(a, b, (dims, ((), ())), preferred_element_type=F32)


def scatter_modes(modes_out, wide_ref, first_row, rows, block_rows, channels, devices):
    half = modes_out.shape[0] // 2
    per_device = half // devices
    lanes = 2 * channels
    low = low_half((half, lanes), channels)
    for pair in range(rows // 2):
        real = modes_out[:half, pair * lanes : (pair + 1) * lanes]
        imag = modes_out[half:, pair * lanes : (pair + 1) * lanes]
        even = jnp.where(low, real, pltpu.roll(imag, channels, 1))
        odd = jnp.where(low, pltpu.roll(real, channels, 1), imag)
        for offset, values in ((0, even), (1, odd)):
            row = first_row + 2 * pair + offset
            for k in range(per_device):
                wide_ref[k, pl.ds(row, devices, stride=block_rows), :] = values[
                    k * devices : (k + 1) * devices
                ]


def gather_modes(wide_ref, first_row, rows, block_rows, channels, devices):
    lanes = 2 * channels
    per_device = wide_ref.shape[0]
    low = low_half((per_device * devices, lanes), channels)
    reals, imags = [], []
    for pair in range(rows // 2):
        even, odd = [
            jnp.concatenate(
                [
                    wide_ref[
                        k, pl.ds(first_row + 2 * pair + offset, devices, stride=block_rows), :
                    ]
                    for k in range(per_device)
                ],
                axis=0,
            )
            for offset in range(2)
        ]
        reals.append(jnp.where(low, even, pltpu.roll(odd, channels, 1)))
        imags.append(jnp.where(low, pltpu.roll(even, channels, 1), odd))
    return jnp.concatenate(
        [jnp.concatenate(reals, axis=1), jnp.concatenate(imags, axis=1)], axis=0
    )


def pack(wide_ref, out_ref):
    lanes = wide_ref.shape[2]
    for k in range(wide_ref.shape[0]):
        out_ref[:, k * lanes : (k + 1) * lanes] = wide_ref[k].astype(BF16)


def unpack(in_ref, wide_ref):
    lanes = wide_ref.shape[2]
    for k in range(wide_ref.shape[0]):
        wide_ref[k] = in_ref[:, k * lanes : (k + 1) * lanes].astype(F32)


def wide_scratch(shape, channels):
    return pltpu.VMEM((shape[1] // (2 * channels), shape[0], 2 * channels), F32)


def in_vmem(array):
    return pltpu.with_memory_space_constraint(array, pltpu.VMEM)


def in_hbm(array):
    return pltpu.with_memory_space_constraint(array, pltpu.HBM)


def params(limit):
    return pltpu.CompilerParams(vmem_limit_bytes=limit * 2**20)


OUTSIDE = pl.BlockSpec(memory_space=pltpu.HBM)
RESIDENT = pl.BlockSpec(memory_space=pltpu.VMEM)


def first_kernel(
    block_rows, channels, devices, rows,
    fields_ref, table_ref, weights_ref, modes_ref, own_ref, copy_ref, table_copy, wide_ref, sems,
):
    steps, block = block_rows // rows, rows * channels
    table_read = pltpu.make_async_copy(table_ref, table_copy, sems.at[steps])
    per_device = own_ref.shape[1]
    own = pl.ds(lax.rem(lax.axis_index("lat"), devices) * per_device, per_device)
    own_read = pltpu.make_async_copy(weights_ref.at[:, own], own_ref, sems.at[steps + 1])

    def read(step):
        part = pl.ds(step * block, block)
        return pltpu.make_async_copy(fields_ref.at[part], copy_ref.at[part], sems.at[step])

    table_read.start()
    for step in range(steps):
        read(step).start()
    own_read.start()
    table_read.wait()

    def body(step, carry):
        read(step).wait()
        field = copy_ref[pl.ds(pl.multiple_of(step * block, block), block), :]
        modes = dot(table_copy[...], field, ((1,), (1,)))
        scatter_modes(modes, wide_ref, step * rows, rows, block_rows, channels, devices)
        return carry

    lax.fori_loop(0, steps, body, 0)
    own_read.wait()
    pack(wide_ref, modes_ref)


def first_transform(fields, table, weights, block_rows, channels, devices, rows):
    per_device = weights.shape[1] // devices
    own_shape = (weights.shape[0], per_device) + weights.shape[2:]
    modes_shape = (devices * block_rows, table.shape[0] // devices * channels)
    return pl.pallas_call(
        functools.partial(first_kernel, block_rows, channels, devices, rows),
        in_specs=[OUTSIDE, OUTSIDE, OUTSIDE],
        out_specs=[RESIDENT, RESIDENT],
        out_shape=[pltpu.VMEM(modes_shape, BF16), pltpu.VMEM(own_shape, BF16)],
        scratch_shapes=[
            pltpu.VMEM(fields.shape, BF16),
            pltpu.VMEM(table.shape, BF16),
            wide_scratch(modes_shape, channels),
            pltpu.SemaphoreType.DMA((block_rows // rows + 2,)),
        ],
        compiler_params=params(24),
    )(in_hbm(fields), in_hbm(table), in_hbm(weights))


def local_kernel(field_ref, weight_ref, out_ref):
    out_ref[...] = dot(weight_ref[...], field_ref[...], ((1,), (0,))).astype(BF16)


def local_mix(field, weight):
    block = pl.BlockSpec((weight.shape[0], field.shape[1]), lambda g: (g, 0))
    return pl.pallas_call(
        local_kernel,
        grid=(field.shape[0] // weight.shape[0],),
        in_specs=[block, pl.BlockSpec(weight.shape, lambda g: (0, 0))],
        out_specs=block,
        out_shape=pltpu.HBM(field.shape, BF16),
        compiler_params=params(16),
    )(in_hbm(field), weight)


def partial_kernel(channels, first, values_ref, forward_ref, out_ref):
    kept = forward_ref.shape[1] // 2
    lanes = 2 * channels
    half = lax.axis_index("lat") * forward_ref.shape[0] // lax.axis_size("lat")
    columns = slice(first * lanes, first * lanes + out_ref.shape[1])
    products = dot(forward_ref[half], values_ref[:, columns], ((1,), (0,)))
    low = low_half((kept, lanes), channels)
    for start in range(0, out_ref.shape[1], lanes):
        part = slice(start, start + lanes)
        turned = pltpu.roll(products[kept:, part], channels, 1)
        sums = products[:kept, part] + jnp.where(low, turned, -turned)
        out_ref[:, part] = sums.astype(BF16)


def partial_sums(values, forward, first, count, channels):
    shape = (forward.shape[1] // 2, count * 2 * channels)
    return pl.pallas_call(
        functools.partial(partial_kernel, channels, first),
        in_specs=[RESIDENT] * 2,
        out_specs=RESIDENT,
        out_shape=jax.ShapeDtypeStruct(shape, BF16),
        compiler_params=params(24),
    )(in_vmem(values), in_vmem(forward))


def middle_kernel(
    channels, layer, first, own_ref, other_ref, weights_ref, backward_ref, *rest
):
    out_ref, copy_ref, sems = rest[-3:]
    kept = own_ref.shape[0]
    lanes = 2 * channels
    half = lax.axis_index("lat") * backward_ref.shape[0] // lax.axis_size("lat")
    low = low_half((kept, lanes), channels)
    low_w = low_half((channels, lanes), channels)
    writes = []
    for k in range(own_ref.shape[1] // lanes):
        part = slice(k * lanes, (k + 1) * lanes)
        modes = (own_ref[:, part].astype(F32) + other_ref[:, part].astype(F32)).astype(BF16)
        weight = weights_ref[layer, first + k].astype(F32)
        swapped = pltpu.roll(weight, channels, 1)
        mixing = jnp.concatenate([weight, jnp.where(low_w, -swapped, swapped)], axis=0)
        mixed = dot(modes, mixing.astype(BF16), ((1,), (0,)))
        swapped = pltpu.roll(mixed, channels, 1)
        both = jnp.concatenate([mixed, jnp.where(low, -swapped, swapped)], axis=0).astype(BF16)
        copy_ref[k] = dot(backward_ref[half], both, ((1,), (0,))).astype(BF16)
        target = out_ref.at[:, pl.ds((first + k) * lanes, lanes)]
        writes.append(pltpu.make_async_copy(copy_ref.at[k], target, sems.at[k]))
        writes[-1].start()
    for write in writes:
        write.wait()


def middle(own, other, weights, layer, first, backward, so_far, channels):
    count = own.shape[1] // (2 * channels)
    rows = backward.shape[1]
    args = [in_vmem(own), in_vmem(other), in_vmem(weights), in_vmem(backward)]
    specs = [RESIDENT] * 4
    if so_far is not None:
        args.append(in_hbm(so_far))
        specs.append(OUTSIDE)
    return pl.pallas_call(
        functools.partial(middle_kernel, channels, layer, first),
        in_specs=specs,
        out_specs=OUTSIDE,
        out_shape=pltpu.HBM((rows, weights.shape[1] * 2 * channels), BF16),
        scratch_shapes=[
            pltpu.VMEM((count, rows, 2 * channels), BF16),
            pltpu.SemaphoreType.DMA((count,)),
        ],
        input_output_aliases={} if so_far is None else {4: 0},
        compiler_params=params(24),
    )(*args)


def gelu_of_double(v):
    scale = math.sqrt(2.0 / math.pi)
    return v * jnp.tanh(v * (BF16(2.0 * scale) + BF16(8.0 * 0.044715 * scale) * (v * v))) + v


def back_kernel(
    block_rows, channels, devices, rows, kind, modes_ref, local_ref, back_ref, *rest
):
    if kind == "field":
        out_ref, *rest = rest
    else:
        extra_ref, out_ref, *rest = rest
    local_copy, field_ref, wide_ref, lhs_ref, in_sems, out_sems, *rest = rest
    steps, block = block_rows // rows, rows * channels
    lon_count = back_ref.shape[1]
    chunk = min(256, lon_count)

    def arriving(step):
        part = pl.ds(step * block, block)
        return pltpu.make_async_copy(local_ref.at[part], local_copy.at[part], in_sems.at[step])

    def leaving(step):
        part = pl.ds(step * block, block)
        return pltpu.make_async_copy(field_ref.at[part], out_ref.at[part], out_sems.at[step])

    for step in range(steps):
        arriving(step).start()
    if kind == "modes":
        wide_out_ref, table_ref, table_sem = rest
        table_read = pltpu.make_async_copy(extra_ref, table_ref, table_sem)
        table_read.start()
    unpack(modes_ref, wide_ref)
    few = math.gcd(rows, max(2, 256 // channels))

    def relayout(step, carry):
        modes = gather_modes(wide_ref, step * few, few, block_rows, channels, devices)
        size = few * channels
        lhs_ref[pl.ds(pl.multiple_of(step * size, size), size), :] = modes.T.astype(BF16)
        return carry

    lax.fori_loop(0, block_rows // few, relayout, 0)

    def body(step, carry):
        first = step * block if isinstance(step, int) else pl.multiple_of(step * block, block)
        part = pl.ds(first, block)
        arriving(step).wait()
        for start in range(0, lon_count, chunk):
            lons = slice(start, start + chunk)
            total = dot(lhs_ref[part, :], back_ref[:, lons], ((1,), (0,))).astype(BF16)
            field_ref[part, lons] = gelu_of_double(total + local_copy[part, lons])
        if kind == "modes":
            if step == 0:
                table_read.wait()
            product = dot(table_ref[...], field_ref[part, :], ((1,), (1,)))
            scatter_modes(product, wide_out_ref, step * rows, rows, block_rows, channels, devices)
        if kind == "mix":
            unit = extra_ref.shape[0]
            for start in range(0, block, unit):
                piece = pl.ds(first + start, unit)
                mixed = dot(extra_ref[...], field_ref[piece, :], ((1,), (0,)))
                field_ref[piece, :] = mixed.astype(BF16)
        if kind != "modes":
            leaving(step).start()
        return carry

    if kind == "field":
        lax.fori_loop(0, steps, body, 0)
    else:
        for step in range(steps):
            body(step, 0)
    if kind == "modes":
        pack(wide_out_ref, out_ref)
    else:
        for step in range(steps):
            leaving(step).wait()


def back_transform(kind, modes, local, back, extra, block_rows, channels, devices, rows):
    steps = block_rows // rows
    scratch = [
        pltpu.VMEM(local.shape, BF16),
        pltpu.VMEM(local.shape, BF16),
        wide_scratch(modes.shape, channels),
        pltpu.VMEM((local.shape[0], back.shape[0]), BF16),
        pltpu.SemaphoreType.DMA((steps,)),
        pltpu.SemaphoreType.DMA((steps,)),
    ]
    args = [in_vmem(modes), in_hbm(local), in_vmem(back)]
    specs = [RESIDENT, OUTSIDE, RESIDENT]
    if kind == "mix":
        args.append(in_vmem(extra))
        specs.append(RESIDENT)
    if kind == "modes":
        args.append(in_hbm(extra))
        specs.append(OUTSIDE)
        scratch.append(wide_scratch(modes.shape, channels))
        scratch.append(pltpu.VMEM(extra.shape, BF16))
        scratch.append(pltpu.SemaphoreType.DMA(()))
    return pl.pallas_call(
        functools.partial(back_kernel, block_rows, channels, devices, rows, kind),
        in_specs=specs,
        out_specs=RESIDENT if kind == "modes" else OUTSIDE,
        out_shape=pltpu.VMEM(modes.shape, BF16)
        if kind == "modes"
        else pltpu.HBM(local.shape, BF16),
        scratch_shapes=scratch,
        compiler_params=params(32),
    )(*args)


def exchange(array, peers, devices):
    parts = array.reshape(peers, array.shape[0] // peers, array.shape[1])
    groups = [list(range(start, start + peers)) for start in range(0, devices, peers)]
    moved = lax.all_to_all(parts, "lat", 0, 0, tiled=True, axis_index_groups=groups)
    return moved.reshape(array.shape)


def shards(fields, spectral_weight, local_weight):
    block_rows, channels, lon_count = fields.shape
    layer_count, mode_count = spectral_weight.shape[:2]
    devices = lax.axis_size("lat")
    rows = max(2, 256 // channels)
    peers = devices // 2
    per_device = mode_count // peers
    counts = [per_device - per_device // 2, per_device // 2]
    swap = [(source, (source + peers) % devices) for source in range(devices)]
    forward_lon, backward_lon = lon_tables(lon_count, mode_count, peers)
    forward_lat, backward_lat = lat_tables(block_rows * devices, KY, block_rows)
    forward_lat = np.stack(np.split(forward_lat, 2, axis=1))
    backward_lat = np.stack(np.split(backward_lat, 2, axis=0))
    mixers = jnp.einsum(
        "rs,lcd->lrdsc", 0.5 * jnp.eye(rows, dtype=BF16), local_weight
    ).reshape(layer_count, rows * channels, rows * channels)
    wide_rows = 2 * rows if block_rows % (2 * rows) == 0 else rows
    sizes = dict(block_rows=block_rows, channels=channels, devices=peers, rows=wide_rows)
    field = fields.reshape(block_rows * channels, lon_count)
    modes, weights = first_transform(field, forward_lon, spectral_weight, **sizes)
    local = local_mix(field, mixers[0])
    for layer in range(layer_count):
        arrived = exchange(modes, peers, devices)
        sums = []
        for first, count in zip((0, counts[0]), counts, strict=True):
            own = partial_sums(arrived, forward_lat, first, count, channels)
            sums.append((first, own, lax.ppermute(own, "lat", swap)))
        rebuilt = None
        for first, own, other in sums:
            rebuilt = middle(own, other, weights, layer, first, backward_lat, rebuilt, channels)
        returned = exchange(rebuilt, peers, devices)
        end = functools.partial(back_transform, modes=returned, local=local, back=backward_lon)
        if layer < layer_count - 1:
            modes = end("modes", extra=forward_lon, **sizes)
            local = end("mix", extra=mixers[layer + 1], **sizes)
        else:
            field = end("field", extra=None, **{**sizes, "rows": rows})
    return field.reshape(fields.shape)


def solution(mesh):
    return jax.shard_map(
        shards,
        mesh=mesh,
        in_specs=(P(("grp", "lat"), None, None), P(), P()),
        out_specs=P(("grp", "lat"), None, None),
        check_vma=False,
    )
```

```python
import functools
import math

import jax
import jax.numpy as jnp
import ml_dtypes
import numpy as np
from jax import lax
from jax.experimental import pallas as pl
from jax.experimental.pallas import tpu as pltpu
from jax.sharding import PartitionSpec as P

KY = 128
F32 = jnp.float32
BF16 = jnp.bfloat16


def rounded(table):
    return np.asarray(table, np.float32).astype(ml_dtypes.bfloat16)


def mode_order(mode_count, devices):
    per_device = mode_count // devices
    return np.arange(mode_count).reshape(devices, per_device).T.reshape(-1)


def lon_tables(lon_count, mode_count, devices):
    modes = mode_order(mode_count, devices).astype(np.int64)[:, None]
    cells = np.arange(lon_count, dtype=np.int64)[None, :]
    angle = 2.0 * np.pi / lon_count * (cells * modes % lon_count)
    both = np.concatenate([np.cos(angle), -np.sin(angle)], axis=0)
    return (rounded(both / math.sqrt(lon_count)), rounded(both / math.sqrt(mode_count) * 0.5))


def lat_tables(lat_count, kept_count, block_rows):
    index = np.arange(kept_count, dtype=np.int64)
    waves = np.where(index < kept_count // 2, index, lat_count - kept_count + index)
    rowids = np.arange(lat_count, dtype=np.int64)
    latitudes = rowids % block_rows * (lat_count // block_rows) + rowids // block_rows
    angle = 2.0 * np.pi / lat_count * (waves[:, None] * latitudes[None, :] % lat_count)
    both = np.concatenate([np.cos(angle), np.sin(angle)], axis=0)
    return (rounded(both / math.sqrt(lat_count)), rounded(both.T / math.sqrt(kept_count)))


def low_half(shape, channels):
    return lax.broadcasted_iota(jnp.int32, shape, len(shape) - 1) % (2 * channels) < channels


def dot(a, b, dims):
    return lax.dot_general(a, b, (dims, ((), ())), preferred_element_type=F32)


def scatter_modes(modes_out, wide_ref, first_row, rows, block_rows, channels, devices):
    half = modes_out.shape[0] // 2
    per_device = half // devices
    lanes = 2 * channels
    low = low_half((half, lanes), channels)
    for pair in range(rows // 2):
        real = modes_out[:half, pair * lanes : (pair + 1) * lanes]
        imag = modes_out[half:, pair * lanes : (pair + 1) * lanes]
        even = jnp.where(low, real, pltpu.roll(imag, channels, 1))
        odd = jnp.where(low, pltpu.roll(real, channels, 1), imag)
        for offset, values in ((0, even), (1, odd)):
            row = first_row + 2 * pair + offset
            for k in range(per_device):
                wide_ref[k, pl.ds(row, devices, stride=block_rows), :] = values[
                    k * devices : (k + 1) * devices
                ]


def gather_modes(wide_ref, first_row, rows, block_rows, channels, devices):
    lanes = 2 * channels
    per_device = wide_ref.shape[0]
    low = low_half((per_device * devices, lanes), channels)
    reals, imags = [], []
    for pair in range(rows // 2):
        even, odd = [
            jnp.concatenate(
                [
                    wide_ref[
                        k, pl.ds(first_row + 2 * pair + offset, devices, stride=block_rows), :
                    ]
                    for k in range(per_device)
                ],
                axis=0,
            )
            for offset in range(2)
        ]
        reals.append(jnp.where(low, even, pltpu.roll(odd, channels, 1)))
        imags.append(jnp.where(low, pltpu.roll(even, channels, 1), odd))
    return jnp.concatenate(
        [jnp.concatenate(reals, axis=1), jnp.concatenate(imags, axis=1)], axis=0
    )


def pack(wide_ref, out_ref):
    lanes = wide_ref.shape[2]
    for k in range(wide_ref.shape[0]):
        out_ref[:, k * lanes : (k + 1) * lanes] = wide_ref[k].astype(BF16)


def unpack(in_ref, wide_ref):
    lanes = wide_ref.shape[2]
    for k in range(wide_ref.shape[0]):
        wide_ref[k] = in_ref[:, k * lanes : (k + 1) * lanes].astype(F32)


def wide_scratch(shape, channels):
    return pltpu.VMEM((shape[1] // (2 * channels), shape[0], 2 * channels), F32)


def in_vmem(array):
    return pltpu.with_memory_space_constraint(array, pltpu.VMEM)


def in_hbm(array):
    return pltpu.with_memory_space_constraint(array, pltpu.HBM)


def params(limit):
    return pltpu.CompilerParams(vmem_limit_bytes=limit * 2**20)


OUTSIDE = pl.BlockSpec(memory_space=pltpu.HBM)
RESIDENT = pl.BlockSpec(memory_space=pltpu.VMEM)


def first_kernel(
    block_rows, channels, devices, rows,
    fields_ref, table_ref, weights_ref, forward_ref, backward_ref,
    modes_ref, own_ref, own_forward, own_backward, copy_ref, table_copy, wide_ref, sems,
):
    steps, block = block_rows // rows, rows * channels
    table_read = pltpu.make_async_copy(table_ref, table_copy, sems.at[steps])
    per_device = own_ref.shape[1]
    own = pl.ds(lax.rem(lax.axis_index("lat"), devices) * per_device, per_device)
    half = lax.axis_index("lat") * forward_ref.shape[0] // lax.axis_size("lat")
    own_reads = [
        pltpu.make_async_copy(weights_ref.at[:, own], own_ref, sems.at[steps + 1]),
        pltpu.make_async_copy(forward_ref.at[half], own_forward, sems.at[steps + 2]),
        pltpu.make_async_copy(backward_ref.at[half], own_backward, sems.at[steps + 3]),
    ]

    def read(step):
        part = pl.ds(step * block, block)
        return pltpu.make_async_copy(fields_ref.at[part], copy_ref.at[part], sems.at[step])

    table_read.start()
    for step in range(steps):
        read(step).start()
    for own_read in own_reads:
        own_read.start()
    table_read.wait()

    def body(step, carry):
        read(step).wait()
        field = copy_ref[pl.ds(pl.multiple_of(step * block, block), block), :]
        modes = dot(table_copy[...], field, ((1,), (1,)))
        scatter_modes(modes, wide_ref, step * rows, rows, block_rows, channels, devices)
        return carry

    lax.fori_loop(0, steps, body, 0)
    for own_read in own_reads:
        own_read.wait()
    pack(wide_ref, modes_ref)


def first_transform(fields, table, weights, lat_pair, block_rows, channels, devices, rows):
    per_device = weights.shape[1] // devices
    own_shape = (weights.shape[0], per_device) + weights.shape[2:]
    modes_shape = (devices * block_rows, table.shape[0] // devices * channels)
    return pl.pallas_call(
        functools.partial(first_kernel, block_rows, channels, devices, rows),
        in_specs=[OUTSIDE] * 5,
        out_specs=[RESIDENT] * 4,
        out_shape=[pltpu.VMEM(modes_shape, BF16), pltpu.VMEM(own_shape, BF16)]
        + [pltpu.VMEM(pair.shape[1:], BF16) for pair in lat_pair],
        scratch_shapes=[
            pltpu.VMEM(fields.shape, BF16),
            pltpu.VMEM(table.shape, BF16),
            wide_scratch(modes_shape, channels),
            pltpu.SemaphoreType.DMA((block_rows // rows + 4,)),
        ],
        compiler_params=params(24),
    )(*[in_hbm(array) for array in (fields, table, weights, *lat_pair)])


def local_kernel(field_ref, weight_ref, out_ref):
    out_ref[...] = dot(weight_ref[...], field_ref[...], ((1,), (0,))).astype(BF16)


def local_mix(field, weight):
    block = pl.BlockSpec((weight.shape[0], field.shape[1]), lambda g: (g, 0))
    return pl.pallas_call(
        local_kernel,
        grid=(field.shape[0] // weight.shape[0],),
        in_specs=[block, pl.BlockSpec(weight.shape, lambda g: (0, 0))],
        out_specs=block,
        out_shape=pltpu.HBM(field.shape, BF16),
        compiler_params=params(16),
    )(in_hbm(field), weight)


def partial_kernel(channels, first, values_ref, forward_ref, out_ref):
    kept = forward_ref.shape[0] // 2
    lanes = 2 * channels
    columns = slice(first * lanes, first * lanes + out_ref.shape[1])
    products = dot(forward_ref[...], values_ref[:, columns], ((1,), (0,)))
    low = low_half((kept, lanes), channels)
    for start in range(0, out_ref.shape[1], lanes):
        part = slice(start, start + lanes)
        turned = pltpu.roll(products[kept:, part], channels, 1)
        sums = products[:kept, part] + jnp.where(low, turned, -turned)
        out_ref[:, part] = sums.astype(BF16)


def partial_sums(values, forward, first, count, channels):
    shape = (forward.shape[0] // 2, count * 2 * channels)
    return pl.pallas_call(
        functools.partial(partial_kernel, channels, first),
        in_specs=[RESIDENT] * 2,
        out_specs=RESIDENT,
        out_shape=jax.ShapeDtypeStruct(shape, BF16),
        compiler_params=params(24),
    )(in_vmem(values), in_vmem(forward))


def middle_kernel(
    channels, layer, first, own_ref, other_ref, weights_ref, backward_ref, *rest
):
    out_ref, copy_ref, sems = rest[-3:]
    kept = own_ref.shape[0]
    lanes = 2 * channels
    low = low_half((kept, lanes), channels)
    low_w = low_half((channels, lanes), channels)
    writes = []
    for k in range(own_ref.shape[1] // lanes):
        part = slice(k * lanes, (k + 1) * lanes)
        modes = (own_ref[:, part].astype(F32) + other_ref[:, part].astype(F32)).astype(BF16)
        weight = weights_ref[layer, first + k].astype(F32)
        swapped = pltpu.roll(weight, channels, 1)
        mixing = jnp.concatenate([weight, jnp.where(low_w, -swapped, swapped)], axis=0)
        mixed = dot(modes, mixing.astype(BF16), ((1,), (0,)))
        swapped = pltpu.roll(mixed, channels, 1)
        both = jnp.concatenate([mixed, jnp.where(low, -swapped, swapped)], axis=0).astype(BF16)
        copy_ref[k] = dot(backward_ref[...], both, ((1,), (0,))).astype(BF16)
        target = out_ref.at[:, pl.ds((first + k) * lanes, lanes)]
        writes.append(pltpu.make_async_copy(copy_ref.at[k], target, sems.at[k]))
        writes[-1].start()
    for write in writes:
        write.wait()


def middle(own, other, weights, layer, first, backward, so_far, channels):
    count = own.shape[1] // (2 * channels)
    rows = backward.shape[0]
    args = [in_vmem(own), in_vmem(other), in_vmem(weights), in_vmem(backward)]
    specs = [RESIDENT] * 4
    if so_far is not None:
        args.append(in_hbm(so_far))
        specs.append(OUTSIDE)
    return pl.pallas_call(
        functools.partial(middle_kernel, channels, layer, first),
        in_specs=specs,
        out_specs=OUTSIDE,
        out_shape=pltpu.HBM((rows, weights.shape[1] * 2 * channels), BF16),
        scratch_shapes=[
            pltpu.VMEM((count, rows, 2 * channels), BF16),
            pltpu.SemaphoreType.DMA((count,)),
        ],
        input_output_aliases={} if so_far is None else {4: 0},
        compiler_params=params(24),
    )(*args)


def gelu_of_double(v):
    scale = math.sqrt(2.0 / math.pi)
    return v * jnp.tanh(v * (BF16(2.0 * scale) + BF16(8.0 * 0.044715 * scale) * (v * v))) + v


def back_kernel(
    block_rows, channels, devices, rows, kind, modes_ref, local_ref, back_ref, *rest
):
    if kind == "field":
        out_ref, *rest = rest
    else:
        extra_ref, out_ref, *rest = rest
    local_copy, field_ref, wide_ref, lhs_ref, in_sems, out_sems, *rest = rest
    steps, block = block_rows // rows, rows * channels
    lon_count = back_ref.shape[1]
    chunk = min(256, lon_count)

    def arriving(step):
        part = pl.ds(step * block, block)
        return pltpu.make_async_copy(local_ref.at[part], local_copy.at[part], in_sems.at[step])

    def leaving(step):
        part = pl.ds(step * block, block)
        return pltpu.make_async_copy(field_ref.at[part], out_ref.at[part], out_sems.at[step])

    for step in range(steps):
        arriving(step).start()
    unpack(modes_ref, wide_ref)
    few = math.gcd(rows, max(2, 256 // channels))

    def relayout(step, carry):
        modes = gather_modes(wide_ref, step * few, few, block_rows, channels, devices)
        size = few * channels
        lhs_ref[pl.ds(pl.multiple_of(step * size, size), size), :] = modes.T.astype(BF16)
        return carry

    lax.fori_loop(0, block_rows // few, relayout, 0)

    def body(step, carry):
        first = step * block if isinstance(step, int) else pl.multiple_of(step * block, block)
        part = pl.ds(first, block)
        arriving(step).wait()
        for start in range(0, lon_count, chunk):
            lons = slice(start, start + chunk)
            total = dot(lhs_ref[part, :], back_ref[:, lons], ((1,), (0,))).astype(BF16)
            field_ref[part, lons] = gelu_of_double(total + local_copy[part, lons])
        if kind == "modes":
            product = dot(extra_ref[...], field_ref[part, :], ((1,), (1,)))
            scatter_modes(product, rest[0], step * rows, rows, block_rows, channels, devices)
        if kind == "mix":
            unit = extra_ref.shape[0]
            for start in range(0, block, unit):
                piece = pl.ds(first + start, unit)
                mixed = dot(extra_ref[...], field_ref[piece, :], ((1,), (0,)))
                field_ref[piece, :] = mixed.astype(BF16)
        if kind != "modes":
            leaving(step).start()
        return carry

    if kind == "field":
        lax.fori_loop(0, steps, body, 0)
    else:
        for step in range(steps):
            body(step, 0)
    if kind == "modes":
        pack(rest[0], out_ref)
    else:
        for step in range(steps):
            leaving(step).wait()


def back_transform(kind, modes, local, back, extra, block_rows, channels, devices, rows):
    steps = block_rows // rows
    scratch = [
        pltpu.VMEM(local.shape, BF16),
        pltpu.VMEM(local.shape, BF16),
        wide_scratch(modes.shape, channels),
        pltpu.VMEM((local.shape[0], back.shape[0]), BF16),
        pltpu.SemaphoreType.DMA((steps,)),
        pltpu.SemaphoreType.DMA((steps,)),
    ]
    args = [in_vmem(modes), in_hbm(local), in_vmem(back)]
    if kind != "field":
        args.append(in_vmem(extra))
    if kind == "modes":
        scratch.append(wide_scratch(modes.shape, channels))
    return pl.pallas_call(
        functools.partial(back_kernel, block_rows, channels, devices, rows, kind),
        in_specs=[RESIDENT, OUTSIDE] + [RESIDENT] * (len(args) - 2),
        out_specs=RESIDENT if kind == "modes" else OUTSIDE,
        out_shape=pltpu.VMEM(modes.shape, BF16)
        if kind == "modes"
        else pltpu.HBM(local.shape, BF16),
        scratch_shapes=scratch,
        compiler_params=params(32),
    )(*args)


def exchange(array, peers, devices):
    parts = array.reshape(peers, array.shape[0] // peers, array.shape[1])
    groups = [list(range(start, start + peers)) for start in range(0, devices, peers)]
    moved = lax.all_to_all(parts, "lat", 0, 0, tiled=True, axis_index_groups=groups)
    return moved.reshape(array.shape)


def shards(fields, spectral_weight, local_weight):
    block_rows, channels, lon_count = fields.shape
    layer_count, mode_count = spectral_weight.shape[:2]
    devices = lax.axis_size("lat")
    rows = max(2, 256 // channels)
    peers = devices // 2
    per_device = mode_count // peers
    counts = [per_device - per_device // 2, per_device // 2]
    swap = [(source, (source + peers) % devices) for source in range(devices)]
    forward_lon, backward_lon = lon_tables(lon_count, mode_count, peers)
    forward_lat, backward_lat = lat_tables(block_rows * devices, KY, block_rows)
    forward_lat = np.stack(np.split(forward_lat, 2, axis=1))
    backward_lat = np.stack(np.split(backward_lat, 2, axis=0))
    mixers = jnp.einsum(
        "rs,lcd->lrdsc", 0.5 * jnp.eye(rows, dtype=BF16), local_weight
    ).reshape(layer_count, rows * channels, rows * channels)
    wide_rows = 2 * rows if block_rows % (2 * rows) == 0 else rows
    sizes = dict(block_rows=block_rows, channels=channels, devices=peers, rows=wide_rows)
    field = fields.reshape(block_rows * channels, lon_count)
    modes, weights, forward_lat, backward_lat = first_transform(
        field, forward_lon, spectral_weight, (forward_lat, backward_lat), **sizes
    )
    local = local_mix(field, mixers[0])
    for layer in range(layer_count):
        arrived = exchange(modes, peers, devices)
        sums = []
        for first, count in zip((0, counts[0]), counts, strict=True):
            own = partial_sums(arrived, forward_lat, first, count, channels)
            sums.append((first, own, lax.ppermute(own, "lat", swap)))
        rebuilt = None
        for first, own, other in sums:
            rebuilt = middle(own, other, weights, layer, first, backward_lat, rebuilt, channels)
        returned = exchange(rebuilt, peers, devices)
        end = functools.partial(back_transform, modes=returned, local=local, back=backward_lon)
        if layer < layer_count - 1:
            modes = end("modes", extra=forward_lon, **sizes)
            local = end("mix", extra=mixers[layer + 1], **sizes)
        else:
            field = end("field", extra=None, **{**sizes, "rows": rows})
    return field.reshape(fields.shape)


def solution(mesh):
    return jax.shard_map(
        shards,
        mesh=mesh,
        in_specs=(P(("grp", "lat"), None, None), P(), P()),
        out_specs=P(("grp", "lat"), None, None),
        check_vma=False,
    )
```

```python
import functools
import math

import jax
import jax.numpy as jnp
import ml_dtypes
import numpy as np
from jax import lax
from jax.experimental import pallas as pl
from jax.experimental.pallas import tpu as pltpu
from jax.sharding import PartitionSpec as P

KY = 128
F32 = jnp.float32
BF16 = jnp.bfloat16


def rounded(table):
    return np.asarray(table, np.float32).astype(ml_dtypes.bfloat16)


def mode_order(mode_count, devices):
    per_device = mode_count // devices
    return np.arange(mode_count).reshape(devices, per_device).T.reshape(-1)


def lon_tables(lon_count, mode_count, devices):
    modes = mode_order(mode_count, devices).astype(np.int64)[:, None]
    cells = np.arange(lon_count, dtype=np.int64)[None, :]
    angle = 2.0 * np.pi / lon_count * (cells * modes % lon_count)
    both = np.concatenate([np.cos(angle), -np.sin(angle)], axis=0)
    return (rounded(both / math.sqrt(lon_count)), rounded(both / math.sqrt(mode_count) * 0.5))


def lat_tables(lat_count, kept_count, block_rows):
    index = np.arange(kept_count, dtype=np.int64)
    waves = np.where(index < kept_count // 2, index, lat_count - kept_count + index)
    rowids = np.arange(lat_count, dtype=np.int64)
    latitudes = rowids % block_rows * (lat_count // block_rows) + rowids // block_rows
    angle = 2.0 * np.pi / lat_count * (waves[:, None] * latitudes[None, :] % lat_count)
    both = np.concatenate([np.cos(angle), np.sin(angle)], axis=0)
    return (rounded(both / math.sqrt(lat_count)), rounded(both.T / math.sqrt(kept_count)))


def low_half(shape, channels):
    return lax.broadcasted_iota(jnp.int32, shape, len(shape) - 1) % (2 * channels) < channels


def dot(a, b, dims):
    return lax.dot_general(a, b, (dims, ((), ())), preferred_element_type=F32)


def scatter_modes(modes_out, wide_ref, first_row, rows, block_rows, channels, devices):
    half = modes_out.shape[0] // 2
    per_device = half // devices
    lanes = 2 * channels
    low = low_half((half, lanes), channels)
    for pair in range(rows // 2):
        real = modes_out[:half, pair * lanes : (pair + 1) * lanes]
        imag = modes_out[half:, pair * lanes : (pair + 1) * lanes]
        even = jnp.where(low, real, pltpu.roll(imag, channels, 1))
        odd = jnp.where(low, pltpu.roll(real, channels, 1), imag)
        for offset, values in ((0, even), (1, odd)):
            row = first_row + 2 * pair + offset
            for k in range(per_device):
                wide_ref[k, pl.ds(row, devices, stride=block_rows), :] = values[
                    k * devices : (k + 1) * devices
                ]


def gather_modes(wide_ref, first_row, rows, block_rows, channels, devices):
    lanes = 2 * channels
    per_device = wide_ref.shape[0]
    low = low_half((per_device * devices, lanes), channels)
    reals, imags = [], []
    for pair in range(rows // 2):
        even, odd = [
            jnp.concatenate(
                [
                    wide_ref[
                        k, pl.ds(first_row + 2 * pair + offset, devices, stride=block_rows), :
                    ]
                    for k in range(per_device)
                ],
                axis=0,
            )
            for offset in range(2)
        ]
        reals.append(jnp.where(low, even, pltpu.roll(odd, channels, 1)))
        imags.append(jnp.where(low, pltpu.roll(even, channels, 1), odd))
    return jnp.concatenate(
        [jnp.concatenate(reals, axis=1), jnp.concatenate(imags, axis=1)], axis=0
    )


def pack(wide_ref, out_ref):
    lanes = wide_ref.shape[2]
    for k in range(wide_ref.shape[0]):
        out_ref[:, k * lanes : (k + 1) * lanes] = wide_ref[k].astype(BF16)


def unpack(in_ref, wide_ref):
    lanes = wide_ref.shape[2]
    for k in range(wide_ref.shape[0]):
        wide_ref[k] = in_ref[:, k * lanes : (k + 1) * lanes].astype(F32)


def wide_scratch(shape, channels):
    return pltpu.VMEM((shape[1] // (2 * channels), shape[0], 2 * channels), F32)


def in_vmem(array):
    return pltpu.with_memory_space_constraint(array, pltpu.VMEM)


def in_hbm(array):
    return pltpu.with_memory_space_constraint(array, pltpu.HBM)


def params(limit):
    return pltpu.CompilerParams(vmem_limit_bytes=limit * 2**20)


OUTSIDE = pl.BlockSpec(memory_space=pltpu.HBM)
RESIDENT = pl.BlockSpec(memory_space=pltpu.VMEM)


def first_kernel(
    block_rows, channels, devices, rows,
    fields_ref, table_ref, weights_ref, forward_ref, backward_ref,
    modes_ref, own_ref, own_forward, own_backward, copy_ref, table_copy, wide_ref, sems,
):
    steps, block = block_rows // rows, rows * channels
    table_read = pltpu.make_async_copy(table_ref, table_copy, sems.at[steps])
    per_device = own_ref.shape[1]
    own = pl.ds(lax.rem(lax.axis_index("lat"), devices) * per_device, per_device)
    half = lax.axis_index("lat") * forward_ref.shape[0] // lax.axis_size("lat")
    own_reads = [
        pltpu.make_async_copy(weights_ref.at[:, own], own_ref, sems.at[steps + 1]),
        pltpu.make_async_copy(forward_ref.at[half], own_forward, sems.at[steps + 2]),
        pltpu.make_async_copy(backward_ref.at[half], own_backward, sems.at[steps + 3]),
    ]

    def read(step):
        part = pl.ds(step * block, block)
        return pltpu.make_async_copy(fields_ref.at[part], copy_ref.at[part], sems.at[step])

    table_read.start()
    for step in range(steps):
        read(step).start()
    for own_read in own_reads:
        own_read.start()
    table_read.wait()

    def body(step, carry):
        read(step).wait()
        field = copy_ref[pl.ds(pl.multiple_of(step * block, block), block), :]
        modes = dot(table_copy[...], field, ((1,), (1,)))
        scatter_modes(modes, wide_ref, step * rows, rows, block_rows, channels, devices)
        return carry

    lax.fori_loop(0, steps, body, 0)
    for own_read in own_reads:
        own_read.wait()
    pack(wide_ref, modes_ref)


def first_transform(fields, table, weights, lat_pair, block_rows, channels, devices, rows):
    per_device = weights.shape[1] // devices
    own_shape = (weights.shape[0], per_device) + weights.shape[2:]
    modes_shape = (devices * block_rows, table.shape[0] // devices * channels)
    return pl.pallas_call(
        functools.partial(first_kernel, block_rows, channels, devices, rows),
        in_specs=[OUTSIDE] * 5,
        out_specs=[RESIDENT] * 4,
        out_shape=[pltpu.VMEM(modes_shape, BF16), pltpu.VMEM(own_shape, BF16)]
        + [pltpu.VMEM(pair.shape[1:], BF16) for pair in lat_pair],
        scratch_shapes=[
            pltpu.VMEM(fields.shape, BF16),
            pltpu.VMEM(table.shape, BF16),
            wide_scratch(modes_shape, channels),
            pltpu.SemaphoreType.DMA((block_rows // rows + 4,)),
        ],
        compiler_params=params(24),
    )(*[in_hbm(array) for array in (fields, table, weights, *lat_pair)])


def local_kernel(field_ref, weight_ref, out_ref):
    out_ref[...] = dot(weight_ref[...], field_ref[...], ((1,), (0,))).astype(BF16)


def local_mix(field, weight):
    block = pl.BlockSpec((weight.shape[0], field.shape[1]), lambda g: (g, 0))
    return pl.pallas_call(
        local_kernel,
        grid=(field.shape[0] // weight.shape[0],),
        in_specs=[block, pl.BlockSpec(weight.shape, lambda g: (0, 0))],
        out_specs=block,
        out_shape=pltpu.HBM(field.shape, BF16),
        compiler_params=params(16),
    )(in_hbm(field), weight)


def partial_kernel(channels, first, values_ref, forward_ref, out_ref):
    kept = forward_ref.shape[0] // 2
    lanes = 2 * channels
    columns = slice(first * lanes, first * lanes + out_ref.shape[1])
    products = dot(forward_ref[...], values_ref[:, columns], ((1,), (0,)))
    low = low_half((kept, lanes), channels)
    for start in range(0, out_ref.shape[1], lanes):
        part = slice(start, start + lanes)
        turned = pltpu.roll(products[kept:, part], channels, 1)
        sums = products[:kept, part] + jnp.where(low, turned, -turned)
        out_ref[:, part] = sums.astype(BF16)


def partial_sums(values, forward, first, count, channels):
    shape = (forward.shape[0] // 2, count * 2 * channels)
    return pl.pallas_call(
        functools.partial(partial_kernel, channels, first),
        in_specs=[RESIDENT] * 2,
        out_specs=RESIDENT,
        out_shape=jax.ShapeDtypeStruct(shape, BF16),
        compiler_params=params(24),
    )(in_vmem(values), in_vmem(forward))


def middle_kernel(
    channels, layer, first, own_ref, other_ref, weights_ref, backward_ref, *rest
):
    out_ref, copy_ref, sems = rest[-3:]
    kept = own_ref.shape[0]
    lanes = 2 * channels
    low = low_half((kept, lanes), channels)
    low_w = low_half((channels, lanes), channels)
    writes, rhs = [], []
    count = own_ref.shape[1] // lanes
    for k in range(count):
        part = slice(k * lanes, (k + 1) * lanes)
        modes = (own_ref[:, part].astype(F32) + other_ref[:, part].astype(F32)).astype(BF16)
        weight = weights_ref[layer, first + k].astype(F32)
        swapped = pltpu.roll(weight, channels, 1)
        mixing = jnp.concatenate([weight, jnp.where(low_w, -swapped, swapped)], axis=0)
        mixed = dot(modes, mixing.astype(BF16), ((1,), (0,)))
        swapped = pltpu.roll(mixed, channels, 1)
        both = jnp.concatenate([mixed, jnp.where(low, -swapped, swapped)], axis=0).astype(BF16)
        rhs.append(both)
    for start in range(0, count, 2):
        pair = rhs[start : start + 2]
        back = dot(backward_ref[...], jnp.concatenate(pair, axis=1), ((1,), (0,))).astype(BF16)
        for k in range(start, start + len(pair)):
            copy_ref[k] = back[:, (k - start) * lanes : (k - start + 1) * lanes]
            target = out_ref.at[:, pl.ds((first + k) * lanes, lanes)]
            writes.append(pltpu.make_async_copy(copy_ref.at[k], target, sems.at[k]))
            writes[-1].start()
    for write in writes:
        write.wait()


def middle(own, other, weights, layer, first, backward, so_far, channels):
    count = own.shape[1] // (2 * channels)
    rows = backward.shape[0]
    args = [in_vmem(own), in_vmem(other), in_vmem(weights), in_vmem(backward)]
    specs = [RESIDENT] * 4
    if so_far is not None:
        args.append(in_hbm(so_far))
        specs.append(OUTSIDE)
    return pl.pallas_call(
        functools.partial(middle_kernel, channels, layer, first),
        in_specs=specs,
        out_specs=OUTSIDE,
        out_shape=pltpu.HBM((rows, weights.shape[1] * 2 * channels), BF16),
        scratch_shapes=[
            pltpu.VMEM((count, rows, 2 * channels), BF16),
            pltpu.SemaphoreType.DMA((count,)),
        ],
        input_output_aliases={} if so_far is None else {4: 0},
        compiler_params=params(24),
    )(*args)


def gelu_of_double(v):
    scale = math.sqrt(2.0 / math.pi)
    return v * jnp.tanh(v * (BF16(2.0 * scale) + BF16(8.0 * 0.044715 * scale) * (v * v))) + v


def back_kernel(
    block_rows, channels, devices, rows, kind, modes_ref, local_ref, back_ref, *rest
):
    if kind == "field":
        out_ref, *rest = rest
    else:
        extra_ref, out_ref, *rest = rest
    local_copy, field_ref, wide_ref, lhs_ref, in_sems, out_sems, *rest = rest
    steps, block = block_rows // rows, rows * channels
    lon_count = back_ref.shape[1]
    chunk = min(256, lon_count)

    def arriving(step):
        part = pl.ds(step * block, block)
        return pltpu.make_async_copy(local_ref.at[part], local_copy.at[part], in_sems.at[step])

    def leaving(step):
        part = pl.ds(step * block, block)
        return pltpu.make_async_copy(field_ref.at[part], out_ref.at[part], out_sems.at[step])

    for step in range(steps):
        arriving(step).start()
    unpack(modes_ref, wide_ref)
    few = math.gcd(rows, max(2, 256 // channels))

    def relayout(step, carry):
        modes = gather_modes(wide_ref, step * few, few, block_rows, channels, devices)
        size = few * channels
        lhs_ref[pl.ds(pl.multiple_of(step * size, size), size), :] = modes.T.astype(BF16)
        return carry

    lax.fori_loop(0, block_rows // few, relayout, 0)

    def body(step, carry):
        first = step * block if isinstance(step, int) else pl.multiple_of(step * block, block)
        part = pl.ds(first, block)
        arriving(step).wait()
        for start in range(0, lon_count, chunk):
            lons = slice(start, start + chunk)
            total = dot(lhs_ref[part, :], back_ref[:, lons], ((1,), (0,))).astype(BF16)
            field_ref[part, lons] = gelu_of_double(total + local_copy[part, lons])
        if kind == "modes":
            product = dot(extra_ref[...], field_ref[part, :], ((1,), (1,)))
            scatter_modes(product, rest[0], step * rows, rows, block_rows, channels, devices)
        if kind == "mix":
            unit = extra_ref.shape[0]
            for start in range(0, block, unit):
                piece = pl.ds(first + start, unit)
                mixed = dot(extra_ref[...], field_ref[piece, :], ((1,), (0,)))
                field_ref[piece, :] = mixed.astype(BF16)
        if kind != "modes":
            leaving(step).start()
        return carry

    if kind == "field":
        lax.fori_loop(0, steps, body, 0)
    else:
        for step in range(steps):
            body(step, 0)
    if kind == "modes":
        pack(rest[0], out_ref)
    else:
        for step in range(steps):
            leaving(step).wait()


def back_transform(kind, modes, local, back, extra, block_rows, channels, devices, rows):
    steps = block_rows // rows
    scratch = [
        pltpu.VMEM(local.shape, BF16),
        pltpu.VMEM(local.shape, BF16),
        wide_scratch(modes.shape, channels),
        pltpu.VMEM((local.shape[0], back.shape[0]), BF16),
        pltpu.SemaphoreType.DMA((steps,)),
        pltpu.SemaphoreType.DMA((steps,)),
    ]
    args = [in_vmem(modes), in_hbm(local), in_vmem(back)]
    if kind != "field":
        args.append(in_vmem(extra))
    if kind == "modes":
        scratch.append(wide_scratch(modes.shape, channels))
    return pl.pallas_call(
        functools.partial(back_kernel, block_rows, channels, devices, rows, kind),
        in_specs=[RESIDENT, OUTSIDE] + [RESIDENT] * (len(args) - 2),
        out_specs=RESIDENT if kind == "modes" else OUTSIDE,
        out_shape=pltpu.VMEM(modes.shape, BF16)
        if kind == "modes"
        else pltpu.HBM(local.shape, BF16),
        scratch_shapes=scratch,
        compiler_params=params(32),
    )(*args)


def exchange(array, peers, devices):
    parts = array.reshape(peers, array.shape[0] // peers, array.shape[1])
    groups = [list(range(start, start + peers)) for start in range(0, devices, peers)]
    moved = lax.all_to_all(parts, "lat", 0, 0, tiled=True, axis_index_groups=groups)
    return moved.reshape(array.shape)


def shards(fields, spectral_weight, local_weight):
    block_rows, channels, lon_count = fields.shape
    layer_count, mode_count = spectral_weight.shape[:2]
    devices = lax.axis_size("lat")
    rows = max(2, 256 // channels)
    peers = devices // 2
    per_device = mode_count // peers
    counts = [per_device - per_device // 2, per_device // 2]
    swap = [(source, (source + peers) % devices) for source in range(devices)]
    forward_lon, backward_lon = lon_tables(lon_count, mode_count, peers)
    forward_lat, backward_lat = lat_tables(block_rows * devices, KY, block_rows)
    forward_lat = np.stack(np.split(forward_lat, 2, axis=1))
    backward_lat = np.stack(np.split(backward_lat, 2, axis=0))
    mixers = jnp.einsum(
        "rs,lcd->lrdsc", 0.5 * jnp.eye(rows, dtype=BF16), local_weight
    ).reshape(layer_count, rows * channels, rows * channels)
    wide_rows = 2 * rows if block_rows % (2 * rows) == 0 else rows
    sizes = dict(block_rows=block_rows, channels=channels, devices=peers, rows=wide_rows)
    field = fields.reshape(block_rows * channels, lon_count)
    modes, weights, forward_lat, backward_lat = first_transform(
        field, forward_lon, spectral_weight, (forward_lat, backward_lat), **sizes
    )
    local = local_mix(field, mixers[0])
    for layer in range(layer_count):
        arrived = exchange(modes, peers, devices)
        sums = []
        for first, count in zip((0, counts[0]), counts, strict=True):
            own = partial_sums(arrived, forward_lat, first, count, channels)
            sums.append((first, own, lax.ppermute(own, "lat", swap)))
        rebuilt = None
        for first, own, other in sums:
            rebuilt = middle(own, other, weights, layer, first, backward_lat, rebuilt, channels)
        returned = exchange(rebuilt, peers, devices)
        end = functools.partial(back_transform, modes=returned, local=local, back=backward_lon)
        if layer < layer_count - 1:
            modes = end("modes", extra=forward_lon, **sizes)
            local = end("mix", extra=mixers[layer + 1], **sizes)
        else:
            field = end("field", extra=None, **{**sizes, "rows": rows})
    return field.reshape(fields.shape)


def solution(mesh):
    return jax.shard_map(
        shards,
        mesh=mesh,
        in_specs=(P(("grp", "lat"), None, None), P(), P()),
        out_specs=P(("grp", "lat"), None, None),
        check_vma=False,
    )
```
